32 devices in a mesh: seq: 8 (over z, x), mp: 4 (over y, core).
Axes of the slice: x: 2, y: 2, z: 4, core: 2. Of those that a mesh axis runs over, the one named last changes fastest.
Arguments:
- inputs: bfloat16 [8192, 7168], P('seq')
- norm_gain: float32 [7168], replicated, may hold values from 0.1 to 1.9
- qkv_weight: bfloat16 [7168, 3, 3584], P('seq', None, 'mp'), may hold values from -0.0625 to 0.0625
- adapter_down: bfloat16 [7168, 128], P('seq'), may hold values from -0.0625 to 0.0625
- adapter_up: bfloat16 [3, 128, 3584], P(None, None, 'mp'), may hold values from -0.5 to 0.5
- out_weight: bfloat16 [3584, 3584], P('mp', 'seq'), may hold values from -0.5 to 0.5
- cache_keys: bfloat16 [16, 256, 3584], P('seq', None, 'mp')
- cache_values: bfloat16 [16, 256, 3584], P('seq', None, 'mp'), may hold values from -6 to 6
- cache_lengths: int32 [4], replicated, may hold values from 1 to 1024, 2560 in all
- block_perm: int32 [16], replicated, may hold values from 0 to 15, each once
Outputs:
- block_out: bfloat16 [8192, 3584], P('seq', 'mp')
The draws below stay inside these ranges and needn't reach their ends.
Inputs may be any that keep to these rules, and one draw needn't show every extreme that they name: `cache_lengths`: each request has at least one cached position, and some request fills all of its 4 blocks. `block_perm`: each logical block appears once.
All inputs are finite; a program needn't handle non-finite values.
Results may differ from the reference program's by a relative error of at most 0.025.
Values may be sent and summed in bfloat16 or wider, within the bound.
No kernel may reach another device: no remote copies, remote signals or barrier semaphores. Data moves between devices by JAX's collectives and lax.ppermute only.
A program may use at most 384 MiB of HBM per device.

```python
import math
import jax
import jax.numpy as jnp
import numpy as np
from jax import lax

D = 3584
D_IN = 7168
HEADS = 16
HD = 224
RANK = 128
REQS = 4
QLEN = 2048
BLK = 256
TOKENS = 8192
NBLK_ALL = 16
MAXB = 4


def draw_inputs(key, part):
    base_key, row_key, col_key = jax.random.split(key, 3)
    array_shape = (TOKENS, D_IN)
    base_draw = jax.random.normal(base_key, array_shape, jnp.float32)
    row_scale = jnp.exp(jax.random.uniform(row_key, (TOKENS, 1), jnp.float32, 0.0, math.log(10.0)))
    col_scale = jnp.exp(jax.random.uniform(col_key, (1, D_IN), jnp.float32, 0.0, math.log(10.0)))
    return (base_draw * row_scale * col_scale).astype(jnp.bfloat16)


def draw_cache_keys(key, part):
    base_key = jax.random.fold_in(key, 0)
    array_shape = (NBLK_ALL, BLK, HEADS * HD)
    base_draw = jax.random.normal(base_key, array_shape, jnp.float32)
    return base_draw.astype(jnp.bfloat16)


def strengthened(drawn, rng, source, target, shards_of, factor):
    owner, partner = [(jnp.arange(drawn.shape[dim]) // (drawn.shape[dim] // shards_of)).reshape([-1 if axis == dim else 1 for axis in range(drawn.ndim)]) for dim in (source, target)]
    chosen = jax.random.permutation(rng, shards_of)[partner]
    strong = (owner == chosen) | (owner == (partner + shards_of // 2) % shards_of)
    return jnp.where(strong, factor * drawn, drawn)


def block_scale(stream_key, dims, cuts, smallest, top_value):
    def one(position, parts):
        steps = jax.random.uniform(jax.random.fold_in(jax.random.fold_in(stream_key, 6), position), (parts,), jnp.float32, smallest / len(cuts), top_value / len(cuts))
        return jnp.repeat(jnp.exp(steps), dims[position] // parts).reshape((-1,) + (1,) * (len(dims) - position - 1))

    loudness = one(*cuts[0])
    for cut in cuts[1:]:
        loudness = loudness * one(*cut)
    return loudness


def profile(number_of, total, most, skew):
    weights = [(1 << 20) // math.isqrt(grade ** skew) + 1 for grade in range(2, number_of + 1)]
    surplus, counts = total - most - (number_of - 1), [1] * (number_of - 1)
    while surplus > 0:
        movable = [i for i in range(number_of - 1) if counts[i] < most]
        mass, budget = sum([weights[i] for i in movable]), surplus
        for i in movable:
            more = min(most - counts[i], max(1, budget * weights[i] // mass), surplus)
            counts[i] = counts[i] + more
            surplus = surplus - more
    return np.array([most] + counts)


def ragged(rng, number_of, total, bound, skew):
    if number_of == 2:
        one = jax.random.randint(rng, (), max(1, total - bound), min(bound, total - 1) + 1)
        return jnp.stack([one, total - one])
    tallies = jnp.asarray(profile(number_of, total, bound, skew), jnp.int32)
    couples = (number_of - 1) // 2
    source_of, sink = tallies[1:1 + 2 * couples:2], tallies[2:2 + 2 * couples:2]
    slack = jnp.minimum(source_of - 1, bound - sink)
    moved = jax.random.randint(jax.random.fold_in(rng, 1), (couples,), 0, 1 << 20) % (slack + 1)
    tallies = tallies.at[1:1 + 2 * couples:2].set(source_of - moved).at[2:2 + 2 * couples:2].set(sink + moved)
    return tallies[jax.random.permutation(jax.random.fold_in(rng, 2), number_of)]


def centred(stream_key, shape, deviation, reach, pieces=(), kind=jnp.bfloat16):
    result = jax.random.normal(stream_key, shape, jnp.float32) * deviation
    if len(pieces) > 0:
        result = block_scale(stream_key, shape, pieces, -0.22, 0.18) * result
    return jnp.clip(result, min=-reach, max=reach).astype(kind)


def heavy_noise(rng, dims, deviation, bound, pieces, heavy, kind=jnp.bfloat16):
    entries = deviation * jax.random.normal(rng, dims, jnp.float32)
    if pieces:
        entries = entries * block_scale(rng, dims, pieces, -0.22, 0.18)
    return jnp.clip(strengthened(entries, jax.random.fold_in(rng, 3), *heavy), -bound, bound).astype(kind)


def setup_inputs(seed: int = 0) -> dict:
    keys = jax.random.split(jax.random.key(seed), 11)
    return {
        "inputs": draw_inputs(jax.random.fold_in(keys[10], 71), 0),
        "norm_gain": jnp.clip(1.0 + 0.18 * jax.random.normal(keys[1], (D_IN,), jnp.float32), 0.1, 1.9),
        "qkv_weight": centred(keys[2], (D_IN, 3, HEADS * HD), D_IN ** -0.5, 0.0625, ((0, 8), (2, 4))),
        "adapter_down": centred(keys[3], (D_IN, RANK), D_IN ** -0.5, 0.0625, ((0, 8),)),
        "adapter_up": centred(keys[4], (3, RANK, HEADS * HD), RANK ** -0.5, 0.5, ((2, 4),)),
        "out_weight": heavy_noise(keys[5], (HEADS * HD, D), HD ** -0.5, 0.5, ((0, 4), (1, 8)), (0, 1, 8, 2.0)),
        "cache_keys": draw_cache_keys(jax.random.fold_in(keys[10], 71), 0),
        "cache_values": centred(keys[7], (NBLK_ALL, BLK, HEADS * HD), 1.0, 6.0, ((0, 8), (2, 4))),
        "cache_lengths": ragged(keys[8], REQS, MAXB * BLK * REQS * 5 // 8, MAXB * BLK, 2).astype(jnp.int32),
        "block_perm": jax.random.permutation(keys[9], NBLK_ALL).astype(jnp.int32),
    }


lowest = -1e+30

def reference(inputs, norm_gain, qkv_weight, adapter_down, adapter_up, out_weight, cache_keys, cache_values, cache_lengths, block_perm):
    widened = inputs.astype(jnp.float32)
    normed = (widened * lax.rsqrt(lax.optimization_barrier(jnp.mean(widened * widened, axis=-1, keepdims=True)) + 1e-05) * norm_gain).astype(jnp.bfloat16)
    low_rank = jnp.dot(normed, adapter_down, preferred_element_type=jnp.float32).astype(jnp.bfloat16)
    main_part = jnp.dot(normed, qkv_weight.reshape(D_IN, 3 * HEADS * HD), preferred_element_type=jnp.float32).reshape(TOKENS, 3, HEADS * HD)
    extra = jnp.einsum('tr,krc->tkc', low_rank.astype(jnp.float32), adapter_up.astype(jnp.float32))
    projected = (main_part + extra).astype(jnp.bfloat16)
    max_blocks = NBLK_ALL // REQS
    cache_span = max_blocks * BLK
    inverse = jnp.zeros((NBLK_ALL,), jnp.int32).at[block_perm].set(jnp.arange(NBLK_ALL, dtype=jnp.int32))
    logical_keys = cache_keys[inverse].reshape(REQS, cache_span, HEADS, HD)
    logical_values = cache_values[inverse].reshape(REQS, cache_span, HEADS, HD)
    scale = HD ** (-0.5)

    def one_slot(slot_index):
        request = slot_index
        length = cache_lengths[request]
        rows = lax.dynamic_slice_in_dim(projected, (slot_index * QLEN).astype(jnp.int32), QLEN, 0)
        key_rows = jnp.concatenate([logical_keys[request], rows[:, 1].reshape(QLEN, HEADS, HD)], axis=0)
        value_rows = jnp.concatenate([logical_values[request], rows[:, 2].reshape(QLEN, HEADS, HD)], axis=0)
        cache_ids = jnp.arange(cache_span, dtype=jnp.int32)
        query_pos = length + jnp.arange(QLEN, dtype=jnp.int32)
        key_pos = jnp.concatenate([cache_ids, query_pos])
        key_live = jnp.concatenate([cache_ids < length, jnp.ones((QLEN,), dtype=bool)])
        visible = key_live[None, :] & (key_pos[None, :] <= query_pos[:, None])
        query_rows = rows[:, 0].reshape(QLEN, HEADS, HD)

        def one_head(operands):
            head_queries, head_keys, head_values = operands
            scores = jnp.dot(head_queries, head_keys.T, preferred_element_type=jnp.float32) * scale
            scores = jnp.where(visible, scores, lowest)
            largest = lax.optimization_barrier(jnp.max(scores, axis=-1, keepdims=True))
            weights = jnp.where(visible, jnp.exp(scores - largest), 0.0)
            weight_sum = lax.optimization_barrier(jnp.sum(weights, axis=-1, keepdims=True))
            mixed = jnp.dot(weights.astype(jnp.bfloat16), head_values, preferred_element_type=jnp.float32)
            return (mixed / weight_sum).astype(jnp.bfloat16)
        per_head = lax.map(one_head, (query_rows.transpose(1, 0, 2), key_rows.transpose(1, 0, 2), value_rows.transpose(1, 0, 2)))
        return per_head.transpose(1, 0, 2).reshape(QLEN, HEADS * HD)
    attended = lax.map(one_slot, jnp.arange(REQS, dtype=jnp.int32)).reshape(TOKENS, HEADS * HD)
    return jnp.dot(attended, out_weight, preferred_element_type=jnp.float32).astype(jnp.bfloat16)
```

```python
import jax
import jax.numpy as jnp
from jax import lax
from jax.experimental import pallas as pl
from jax.experimental.pallas import tpu as pltpu
from jax.sharding import PartitionSpec as P

HD = 224
REQS = 4
QLEN = 2048


lowest = -1e30


def lookup(small_table, positions_of):
    hits = positions_of[..., None] == jnp.arange(small_table.shape[0], dtype=jnp.int32)
    return jnp.sum(jnp.where(hits, small_table, 0), axis=-1)


def query_meta(token_index, lengths):
    request = token_index // QLEN
    return (request, lookup(lengths, request) + token_index % QLEN)


def key_meta(row_index, layout, permutation, lengths):
    cache_rows, block_size, tok_dev, max_blocks = layout
    rows_dev = cache_rows + tok_dev
    device = row_index // rows_dev
    local_row = row_index % rows_dev
    block_index = (
        device * (cache_rows // block_size) + jnp.minimum(local_row, cache_rows - 1) // block_size
    )
    logical = lookup(permutation, block_index)
    request = logical // max_blocks
    position = logical % max_blocks * block_size + local_row % block_size
    cached_live = position < lookup(lengths, request)
    new_req, new_pos = query_meta(device * tok_dev + local_row - cache_rows, lengths)
    in_cache = local_row < cache_rows
    key_req = jnp.where(in_cache, jnp.where(cached_live, request, -1), new_req)
    return (key_req, jnp.where(in_cache, position, new_pos))


def attend(softmax_state, queries, query_info, key_rows, value_rows, key_info, head_dim):
    query_req, query_pos = query_info
    key_req, key_pos = key_info
    visible = (key_req[None, :] == query_req[:, None]) & (key_pos[None, :] <= query_pos[:, None])
    query_count = queries.shape[0]
    key_count = key_rows.shape[0]
    head_count = queries.shape[1] // head_dim
    summed, largest, weight_sum = softmax_state
    scores = jnp.einsum(
        "qhd,khd->hqk",
        queries.reshape(query_count, head_count, head_dim),
        key_rows.reshape(key_count, head_count, head_dim),
        preferred_element_type=jnp.float32,
    ) * head_dim ** (-0.5)
    scores = jnp.where(visible[None], scores, lowest)
    new_largest = jnp.maximum(largest, jnp.max(scores, axis=-1))
    weights = jnp.where(visible[None], jnp.exp(scores - new_largest[..., None]), 0.0)
    weight_sum = jnp.sum(weights, axis=-1)
    summed = jnp.einsum(
        "hqk,khd->hqd",
        weights.astype(jnp.bfloat16),
        value_rows.reshape(key_count, head_count, head_dim),
        preferred_element_type=jnp.float32,
    )
    return (summed, new_largest, weight_sum)


def per_device(
    inputs,
    norm_gain,
    qkv_weight,
    adapter_down,
    adapter_up,
    out_weight,
    cache_keys,
    cache_values,
    cache_lengths,
    block_perm,
):
    tok_dev = inputs.shape[0]
    widened = inputs.astype(jnp.float32)
    normed = (
        widened * lax.rsqrt(jnp.mean(widened * widened, axis=-1, keepdims=True) + 1e-05) * norm_gain
    ).astype(jnp.bfloat16)
    head_width = qkv_weight.shape[2]
    weight_rows = lax.all_gather(qkv_weight, "seq", axis=0, tiled=True)
    down_rows = lax.all_gather(adapter_down, "seq", axis=0, tiled=True)
    main_part = jnp.einsum("tr,rkc->ktc", normed, weight_rows, preferred_element_type=jnp.float32)
    low_rank = jnp.dot(normed, down_rows, preferred_element_type=jnp.float32)
    main_part, low_rank = (main_part, low_rank)
    low_rank = low_rank.astype(jnp.bfloat16)
    projected = (
        main_part
        + jnp.einsum("tr,krc->ktc", low_rank, adapter_up, preferred_element_type=jnp.float32)
    ).astype(jnp.bfloat16)
    queries = projected[0]
    new_keys = projected[1]
    new_values = projected[2]
    cycle_index = lax.axis_index("seq")
    cache_rows = cache_keys.shape[0] * cache_keys.shape[1]
    layout = (cache_rows, cache_keys.shape[1], tok_dev, block_perm.shape[0] // REQS)
    key_rows = jnp.concatenate([cache_keys.reshape(cache_rows, head_width), new_keys], axis=0)
    value_rows = jnp.concatenate([cache_values.reshape(cache_rows, head_width), new_values], axis=0)
    token_ids = jnp.arange(tok_dev, dtype=jnp.int32)
    own_info = query_meta(cycle_index * tok_dev + token_ids, cache_lengths)
    head_count = head_width // HD
    softmax_state = (
        jnp.zeros((head_count, tok_dev, HD), jnp.float32),
        jnp.full((head_count, tok_dev), lowest, jnp.float32),
        jnp.zeros((head_count, tok_dev), jnp.float32),
    )
    pieces = (
        lax.all_gather(key_rows, "seq", axis=0, tiled=True),
        lax.all_gather(value_rows, "seq", axis=0, tiled=True),
    )
    row_ids = jnp.arange(pieces[0].shape[0], dtype=jnp.int32)
    key_info = key_meta(row_ids, layout, block_perm, cache_lengths)
    softmax_state = attend(softmax_state, queries, own_info, pieces[0], pieces[1], key_info, HD)
    summed, largest, weight_sum = softmax_state
    attended = (
        (summed / weight_sum[..., None])
        .transpose(1, 0, 2)
        .reshape(tok_dev, head_width)
        .astype(jnp.bfloat16)
    )
    partial_value = jnp.dot(
        attended,
        lax.all_gather(out_weight, "seq", axis=1, tiled=True),
        preferred_element_type=jnp.float32,
    )
    return lax.psum_scatter(
        partial_value.astype(jnp.bfloat16), "mp", scatter_dimension=1, tiled=True
    )


CHUNK = 256
RANK = 128
LOG2E = 1.4426950408889634


def swap(array, axis, size, bit):
    return lax.ppermute(array, axis, [(i, i ^ bit) for i in range(size)])


def pick(array, index, axis=0):
    return lax.dynamic_index_in_dim(array, index, axis, keepdims=False)


def attention_kernel(
    chunk_table, cache_table, lengths, projected_ref, cache_ref, out_ref, total_ref
):
    request = pl.program_id(0)
    tile = pl.program_id(1)
    factor = HD ** (-0.5) * LOG2E

    def chunk_of(number, part):
        return projected_ref[chunk_table[request * 8 + number], pl.ds(part * HD, HD), :]

    queries = jnp.concatenate([chunk_of(2 * tile, 0), chunk_of(2 * tile + 1, 0)], axis=1)
    width = 2 * CHUNK
    total_ref[...] = jnp.zeros_like(total_ref)

    def step(state, keys, values, visible):
        largest, weight_sum = state
        scores = lax.dot_general(
            keys, queries, (((0,), (0,)), ((), ())), preferred_element_type=jnp.float32
        )
        if visible is not None:
            scores = jnp.where(visible, scores, lowest)
        new_largest = jnp.maximum(largest, jnp.max(scores, axis=0, keepdims=True))
        weights = jnp.exp2((scores - new_largest) * factor)
        fade = jnp.exp2((largest - new_largest) * factor)
        weight_sum = weight_sum * fade + jnp.sum(weights, axis=0, keepdims=True)
        total_ref[...] = total_ref[...] * fade + jnp.dot(
            values, weights.astype(jnp.bfloat16), preferred_element_type=jnp.float32
        )
        return (new_largest, weight_sum)

    key_row = lax.broadcasted_iota(jnp.int32, (CHUNK, width), 0)
    query_column = lax.broadcasted_iota(jnp.int32, (CHUNK, width), 1)

    def new_step(number, state):
        return step(state, chunk_of(number, 1), chunk_of(number, 2), None)

    def own_step(number, state):
        visible = key_row + number * CHUNK <= query_column + tile * width
        return step(state, chunk_of(number, 1), chunk_of(number, 2), visible)

    length = lengths[request]

    def cache_step(number, state):
        entry = cache_table[request * 4 + number]
        start = pl.multiple_of((entry % 2) * CHUNK, CHUNK)
        keys = cache_ref[entry // 2, pl.ds(0, HD), pl.ds(start, CHUNK)]
        values = cache_ref[entry // 2, pl.ds(HD, HD), pl.ds(start, CHUNK)]
        return step(state, keys, values, key_row + number * CHUNK < length)

    state = (jnp.full((1, width), lowest, jnp.float32), jnp.zeros((1, width), jnp.float32))
    state = own_step(2 * tile, state)
    state = own_step(2 * tile + 1, state)
    state = lax.fori_loop(0, 2 * tile, new_step, state)
    state = lax.fori_loop(0, pl.cdiv(length, CHUNK), cache_step, state)
    out_ref[...] = (total_ref[...] / state[1]).astype(jnp.bfloat16)[None]


def attention(projected, cached, chunk_table, cache_table, lengths):
    return pl.pallas_call(
        attention_kernel,
        grid_spec=pltpu.PrefetchScalarGridSpec(
            num_scalar_prefetch=3,
            grid=(2, QLEN // (2 * CHUNK)),
            in_specs=[
                pl.BlockSpec(projected.shape, lambda r, i, *_: (0, 0, 0)),
                pl.BlockSpec(cached.shape, lambda r, i, *_: (0, 0, 0)),
            ],
            out_specs=pl.BlockSpec((1, HD, 2 * CHUNK), lambda r, i, *_: (r, 0, i)),
            scratch_shapes=[pltpu.VMEM((HD, 2 * CHUNK), jnp.float32)],
        ),
        out_shape=jax.ShapeDtypeStruct((2, HD, QLEN), jnp.bfloat16),
        compiler_params=pltpu.CompilerParams(vmem_limit_bytes=48 * 2**20),
        cost_estimate=pl.CostEstimate(
            flops=2 * 2 * 2 * QLEN * QLEN * 256,
            bytes_accessed=2 * projected.size,
            transcendentals=2 * QLEN * QLEN,
        ),
    )(chunk_table, cache_table, lengths, projected, cached)


def per_device_paired(
    inputs,
    norm_gain,
    qkv_weight,
    adapter_down,
    adapter_up,
    out_weight,
    cache_keys,
    cache_values,
    cache_lengths,
    block_perm,
):
    tok_dev, width = inputs.shape
    rows = qkv_weight.shape[0]
    seq = lax.axis_index("seq")
    mp = lax.axis_index("mp")
    plane, side = seq // 2, seq % 2
    role = plane % 2

    def over_z(array, bit):
        return swap(array, "seq", 8, 2 * bit)

    def over_x(array):
        return swap(array, "seq", 8, 1)

    def over_y(array):
        return swap(array, "mp", 4, 2)

    def over_core(array):
        return swap(array, "mp", 4, 1)

    widened = inputs.astype(jnp.float32)
    normed = (
        widened * lax.rsqrt(jnp.mean(widened * widened, axis=-1, keepdims=True) + 1e-05) * norm_gain
    ).astype(jnp.bfloat16)

    turned = qkv_weight.reshape(rows, 3, 4, HD).transpose(2, 1, 3, 0).reshape(2, 2, 3 * HD, rows)
    kept = pick(turned, side, 1)
    from_x = over_x(pick(turned, 1 - side, 1))
    weight_blocks = [[pick(kept, role), pick(from_x, role)]]
    for bit in (1, 2, 3):
        other = role ^ (bit & 1)
        weight_blocks.append(
            [over_z(pick(kept, other), bit), over_z(pick(from_x, other), bit)]
        )
    weight_rows = jnp.zeros((3 * HD, width), jnp.bfloat16)
    for bit in range(4):
        for other_side in range(2):
            source = (seq ^ (2 * bit)) ^ other_side
            weight_rows = lax.dynamic_update_slice(
                weight_rows, weight_blocks[bit][other_side], (0, source * rows)
            )

    def turned_cache(cache):
        blocks, size, _ = cache.shape
        return cache.reshape(blocks * size, 4, HD).transpose(1, 2, 0)

    cached = jnp.concatenate([turned_cache(cache_keys), turned_cache(cache_values)], axis=1)
    cached = cached.reshape(2, 2, 2 * HD, cached.shape[2])
    kept_cache = pick(cached, side, 1)
    cache_from_x = over_x(pick(cached, 1 - side, 1))
    cache_blocks = [pick(kept_cache, role), pick(cache_from_x, role)]
    for bit in (1, 2, 3):
        other = role ^ (bit & 1)
        cache_blocks += [
            over_z(pick(kept_cache, other), bit),
            over_z(pick(cache_from_x, other), bit),
        ]
    cached_rows = jnp.stack(cache_blocks)

    part = lax.dynamic_slice_in_dim(normed, mp * CHUNK, CHUNK, 0)
    part_x = over_x(part)
    part_z = over_z(part, 1)
    part_zx = over_x(part_z)

    def completed(piece):
        across = over_y(piece)
        return jnp.concatenate([piece, over_core(piece), across, over_core(across)], axis=0)

    token_sets = [normed, completed(part_x), completed(part_z), completed(part_zx)]

    down_share = lax.dynamic_slice_in_dim(adapter_down, mp * (rows // 4), rows // 4, 0)
    down_rows = lax.all_gather(down_share, ("seq", "mp"), axis=0, tiled=True)
    up = adapter_up.reshape(3, RANK, 4, HD).transpose(2, 0, 3, 1).reshape(4, 3 * HD, RANK)
    up = pick(up, 2 * role + side)

    def project(tokens):
        low_rank = jnp.dot(tokens, down_rows, preferred_element_type=jnp.float32)
        low_rank = low_rank.astype(jnp.bfloat16)
        nt = (((1,), (1,)), ((), ()))
        main_part = lax.dot_general(weight_rows, tokens, nt, preferred_element_type=jnp.float32)
        extra = lax.dot_general(up, low_rank, nt, preferred_element_type=jnp.float32)
        result = (main_part + extra).astype(jnp.bfloat16)
        return result.reshape(3 * HD, 4, CHUNK).transpose(1, 0, 2)

    projected = jnp.concatenate([project(tokens) for tokens in token_sets], axis=0)

    place = jnp.arange(8, dtype=jnp.int32)
    other_side = (place // 4) ^ side
    chunk_table = jnp.concatenate(
        [
            other_side * 4 + jnp.where(other_side == 1, (place % 4) ^ mp, place % 4),
            8 + other_side * 4 + ((place % 4) ^ mp),
        ]
    ).astype(jnp.int32)
    requests = jnp.stack([plane, plane ^ 1])
    lengths = lookup(cache_lengths, requests)
    logical = requests[:, None] * 4 + jnp.arange(4, dtype=jnp.int32)[None, :]
    hits = logical[..., None] == block_perm
    physical = jnp.sum(
        jnp.where(hits, jnp.arange(block_perm.shape[0], dtype=jnp.int32), 0), axis=-1
    ).reshape(8)
    source = (physical // 2) ^ seq
    cache_table = (source * 2 + physical % 2).astype(jnp.int32)

    attended = attention(projected, cached_rows, chunk_table, cache_table, lengths)

    received = over_z(attended[1], 1)
    pair = jnp.where(
        role == 0, jnp.stack([attended[0], received]), jnp.stack([received, attended[0]])
    ).reshape(2, HD, 2, tok_dev)
    mine = pick(pair, side, 2)
    theirs = over_x(pick(pair, 1 - side, 2))
    heads = jnp.where(
        side == 0, jnp.stack([mine, theirs], axis=1), jnp.stack([theirs, mine], axis=1)
    ).reshape(4 * HD, tok_dev)

    out_rows = lax.all_gather(out_weight, "seq", axis=1, tiled=True)
    partial_value = lax.dot_general(
        heads, out_rows, (((0,), (0,)), ((), ())), preferred_element_type=jnp.float32
    ).astype(jnp.bfloat16)
    partial_value = partial_value.reshape(tok_dev, 2, 2, -1)
    core, row = mp % 2, mp // 2
    both = pick(partial_value, core, 2).astype(jnp.float32) + over_core(
        pick(partial_value, 1 - core, 2)
    ).astype(jnp.float32)
    sent = over_y(pick(both, 1 - row, 1).astype(jnp.bfloat16))
    return (pick(both, row, 1) + sent.astype(jnp.float32)).astype(jnp.bfloat16)


def solution(mesh):
    in_specs = (
        P("seq", None),
        P(),
        P("seq", None, "mp"),
        P("seq", None),
        P(None, None, "mp"),
        P("mp", "seq"),
        P("seq", None, "mp"),
        P("seq", None, "mp"),
        P(),
        P(),
    )
    out_specs = P("seq", "mp")
    paired = mesh.shape["seq"] == 8 and mesh.shape["mp"] == 4
    return jax.shard_map(
        per_device_paired if paired else per_device, mesh=mesh, in_specs=in_specs, out_specs=out_specs, check_vma=False
    )
```

```python
import functools

import jax
import jax.numpy as jnp
from jax import lax
from jax.experimental import pallas as pl
from jax.experimental.pallas import tpu as pltpu
from jax.sharding import PartitionSpec as P

HD = 224
REQS = 4
QLEN = 2048


lowest = -1e30


def lookup(small_table, positions_of):
    hits = positions_of[..., None] == jnp.arange(small_table.shape[0], dtype=jnp.int32)
    return jnp.sum(jnp.where(hits, small_table, 0), axis=-1)


def query_meta(token_index, lengths):
    request = token_index // QLEN
    return (request, lookup(lengths, request) + token_index % QLEN)


def key_meta(row_index, layout, permutation, lengths):
    cache_rows, block_size, tok_dev, max_blocks = layout
    rows_dev = cache_rows + tok_dev
    device = row_index // rows_dev
    local_row = row_index % rows_dev
    block_index = (
        device * (cache_rows // block_size) + jnp.minimum(local_row, cache_rows - 1) // block_size
    )
    logical = lookup(permutation, block_index)
    request = logical // max_blocks
    position = logical % max_blocks * block_size + local_row % block_size
    cached_live = position < lookup(lengths, request)
    new_req, new_pos = query_meta(device * tok_dev + local_row - cache_rows, lengths)
    in_cache = local_row < cache_rows
    key_req = jnp.where(in_cache, jnp.where(cached_live, request, -1), new_req)
    return (key_req, jnp.where(in_cache, position, new_pos))


def attend(softmax_state, queries, query_info, key_rows, value_rows, key_info, head_dim):
    query_req, query_pos = query_info
    key_req, key_pos = key_info
    visible = (key_req[None, :] == query_req[:, None]) & (key_pos[None, :] <= query_pos[:, None])
    query_count = queries.shape[0]
    key_count = key_rows.shape[0]
    head_count = queries.shape[1] // head_dim
    summed, largest, weight_sum = softmax_state
    scores = jnp.einsum(
        "qhd,khd->hqk",
        queries.reshape(query_count, head_count, head_dim),
        key_rows.reshape(key_count, head_count, head_dim),
        preferred_element_type=jnp.float32,
    ) * head_dim ** (-0.5)
    scores = jnp.where(visible[None], scores, lowest)
    new_largest = jnp.maximum(largest, jnp.max(scores, axis=-1))
    weights = jnp.where(visible[None], jnp.exp(scores - new_largest[..., None]), 0.0)
    weight_sum = jnp.sum(weights, axis=-1)
    summed = jnp.einsum(
        "hqk,khd->hqd",
        weights.astype(jnp.bfloat16),
        value_rows.reshape(key_count, head_count, head_dim),
        preferred_element_type=jnp.float32,
    )
    return (summed, new_largest, weight_sum)


def per_device(
    inputs,
    norm_gain,
    qkv_weight,
    adapter_down,
    adapter_up,
    out_weight,
    cache_keys,
    cache_values,
    cache_lengths,
    block_perm,
):
    tok_dev = inputs.shape[0]
    widened = inputs.astype(jnp.float32)
    normed = (
        widened * lax.rsqrt(jnp.mean(widened * widened, axis=-1, keepdims=True) + 1e-05) * norm_gain
    ).astype(jnp.bfloat16)
    head_width = qkv_weight.shape[2]
    weight_rows = lax.all_gather(qkv_weight, "seq", axis=0, tiled=True)
    down_rows = lax.all_gather(adapter_down, "seq", axis=0, tiled=True)
    main_part = jnp.einsum("tr,rkc->ktc", normed, weight_rows, preferred_element_type=jnp.float32)
    low_rank = jnp.dot(normed, down_rows, preferred_element_type=jnp.float32)
    main_part, low_rank = (main_part, low_rank)
    low_rank = low_rank.astype(jnp.bfloat16)
    projected = (
        main_part
        + jnp.einsum("tr,krc->ktc", low_rank, adapter_up, preferred_element_type=jnp.float32)
    ).astype(jnp.bfloat16)
    queries = projected[0]
    new_keys = projected[1]
    new_values = projected[2]
    cycle_index = lax.axis_index("seq")
    cache_rows = cache_keys.shape[0] * cache_keys.shape[1]
    layout = (cache_rows, cache_keys.shape[1], tok_dev, block_perm.shape[0] // REQS)
    key_rows = jnp.concatenate([cache_keys.reshape(cache_rows, head_width), new_keys], axis=0)
    value_rows = jnp.concatenate([cache_values.reshape(cache_rows, head_width), new_values], axis=0)
    token_ids = jnp.arange(tok_dev, dtype=jnp.int32)
    own_info = query_meta(cycle_index * tok_dev + token_ids, cache_lengths)
    head_count = head_width // HD
    softmax_state = (
        jnp.zeros((head_count, tok_dev, HD), jnp.float32),
        jnp.full((head_count, tok_dev), lowest, jnp.float32),
        jnp.zeros((head_count, tok_dev), jnp.float32),
    )
    pieces = (
        lax.all_gather(key_rows, "seq", axis=0, tiled=True),
        lax.all_gather(value_rows, "seq", axis=0, tiled=True),
    )
    row_ids = jnp.arange(pieces[0].shape[0], dtype=jnp.int32)
    key_info = key_meta(row_ids, layout, block_perm, cache_lengths)
    softmax_state = attend(softmax_state, queries, own_info, pieces[0], pieces[1], key_info, HD)
    summed, largest, weight_sum = softmax_state
    attended = (
        (summed / weight_sum[..., None])
        .transpose(1, 0, 2)
        .reshape(tok_dev, head_width)
        .astype(jnp.bfloat16)
    )
    partial_value = jnp.dot(
        attended,
        lax.all_gather(out_weight, "seq", axis=1, tiled=True),
        preferred_element_type=jnp.float32,
    )
    return lax.psum_scatter(
        partial_value.astype(jnp.bfloat16), "mp", scatter_dimension=1, tiled=True
    )


CHUNK = 256
GROUP = 128
RANK = 128
LOG2E = 1.4426950408889634


def swap(array, axis, size, bit):
    return lax.ppermute(array, axis, [(i, i ^ bit) for i in range(size)])


def pick(array, index, axis=0):
    return lax.dynamic_index_in_dim(array, index, axis, keepdims=False)


def after(array, *earlier):
    return lax.optimization_barrier((array, *earlier))[0]


def fence(*arrays):
    return lax.optimization_barrier(arrays)


def norm_kernel(first, inputs_ref, gain_ref, out_ref):
    widened = inputs_ref[...].astype(jnp.float32)
    mean = jnp.mean(widened * widened, axis=-1, keepdims=True)
    out_ref[...] = (widened * lax.rsqrt(mean + 1e-05) * gain_ref[...]).astype(jnp.bfloat16)


def normalise(inputs, norm_gain, part, count):
    width = inputs.shape[1]
    rows = 64
    steps = count // rows
    return pl.pallas_call(
        norm_kernel,
        grid_spec=pltpu.PrefetchScalarGridSpec(
            num_scalar_prefetch=1,
            grid=(steps,),
            in_specs=[
                pl.BlockSpec((rows, width), lambda i, first: (first[0] * steps + i, 0)),
                pl.BlockSpec((1, width), lambda i, first: (0, 0)),
            ],
            out_specs=pl.BlockSpec((rows, width), lambda i, first: (i, 0)),
        ),
        out_shape=jax.ShapeDtypeStruct((count, width), jnp.bfloat16),
        compiler_params=pltpu.CompilerParams(vmem_limit_bytes=40 * 2**20),
        cost_estimate=pl.CostEstimate(flops=1, bytes_accessed=1, transcendentals=0),
    )(part.reshape(1), inputs, norm_gain.reshape(1, width))


def project_kernel(sets, order, up_ref, down_ref, *refs):
    token_refs, weight_refs = refs[: len(sets)], refs[len(sets) : -3]
    turned_ref, keys_ref, held_ref = refs[-3:]
    rows = weight_refs[0].shape[1]
    main = 3 * HD
    step = pl.program_id(0)

    @pl.when(step == 0)
    def fill():
        for number, weight_ref in enumerate(weight_refs):
            columns = pl.ds(pl.multiple_of(order[number] * rows, 128), rows)
            held_ref[pl.ds(0, main), columns] = weight_ref[...]
        held_ref[pl.ds(main, RANK), :] = down_ref[...]

    def run(tokens_ref):
        total = lax.dot_general(
            held_ref[...],
            tokens_ref[...],
            (((1,), (1,)), ((), ())),
            preferred_element_type=jnp.float32,
        )
        low_rank = total[main:].astype(jnp.bfloat16)
        total = total[:main] + jnp.dot(up_ref[...], low_rank, preferred_element_type=jnp.float32)
        for number in range(turned_ref.shape[0]):
            columns = slice(number * CHUNK, (number + 1) * CHUNK)
            turned_ref[number, pl.ds(0, HD), :] = total[:HD, columns].astype(jnp.bfloat16)
            turned_ref[number, pl.ds(HD, HD), :] = total[2 * HD :, columns].astype(jnp.bfloat16)
            keys_ref[number] = total[HD : 2 * HD, columns].T.astype(jnp.bfloat16)

    for (first, count), tokens_ref in zip(sets, token_refs):
        pl.when((step >= first) & (step < first + count))(functools.partial(run, tokens_ref))


def project(token_sets, up, down, weight_blocks, order):
    width = token_sets[0].shape[1]
    per_step = 1 if len(token_sets) > 1 else 2
    main = 3 * HD
    sets, steps = [], 0
    for tokens in token_sets:
        sets.append((steps, tokens.shape[0] // (per_step * CHUNK)))
        steps += sets[-1][1]
    chunks = steps * per_step
    whole = lambda array: pl.BlockSpec(array.shape, lambda i, *_: (0,) * array.ndim)

    def token_spec(first, count):
        return pl.BlockSpec(
            (per_step * CHUNK, width), lambda i, *_: (jnp.clip(i - first, 0, count - 1), 0)
        )

    return pl.pallas_call(
        functools.partial(project_kernel, tuple(sets)),
        grid_spec=pltpu.PrefetchScalarGridSpec(
            num_scalar_prefetch=1,
            grid=(steps,),
            in_specs=[whole(array) for array in (up, down)]
            + [token_spec(*one) for one in sets]
            + [
                pl.BlockSpec(
                    (main, array.shape[1]), lambda i, *_: (0, 0), pipeline_mode=pl.Buffered(1)
                )
                for array in weight_blocks
            ],
            out_specs=[
                pl.BlockSpec((per_step, 2 * HD, CHUNK), lambda i, *_: (i, 0, 0)),
                pl.BlockSpec((per_step, CHUNK, HD), lambda i, *_: (i, 0, 0)),
            ],
            scratch_shapes=[pltpu.VMEM((main + RANK, width), jnp.bfloat16)],
        ),
        out_shape=[
            jax.ShapeDtypeStruct((chunks, 2 * HD, CHUNK), jnp.bfloat16),
            jax.ShapeDtypeStruct((chunks, CHUNK, HD), jnp.bfloat16),
        ],
        compiler_params=pltpu.CompilerParams(vmem_limit_bytes=58 * 2**20),
        cost_estimate=pl.CostEstimate(flops=1, bytes_accessed=1, transcendentals=0),
    )(order, up, down, *token_sets, *weight_blocks)


def attention_kernel(
    half,
    chunk_table,
    cache_table,
    length_ref,
    turned_ref,
    keys_ref,
    *refs,
):
    block_refs, (out_ref, total_ref, cached_keys, cached_values) = refs[:-4], refs[-4:]
    tile = 2 * pl.program_id(0) + half
    factor = HD ** (-0.5) * LOG2E
    width = 2 * CHUNK
    length = length_ref[0]

    @pl.when(pl.program_id(0) == 0)
    def gather_cache():
        for number in range(cache_table.shape[0]):
            entry = cache_table[number]
            for bit, block_ref in enumerate(block_refs):

                @pl.when((number * CHUNK < length) & (entry // 4 == bit))
                def take(number=number, entry=entry, block_ref=block_ref):
                    other = (entry // 2) % 2
                    columns = pl.ds(pl.multiple_of((entry % 2) * CHUNK, CHUNK), CHUNK)
                    place = pl.ds(number * CHUNK, CHUNK)
                    keys = block_ref[other, pl.ds(0, HD), columns].astype(jnp.float32)
                    cached_keys[place, :] = keys.T.astype(jnp.bfloat16)
                    cached_values[:, place] = block_ref[other, pl.ds(HD, HD), columns]

    def joined(ref, first, rows):
        pieces = [ref[chunk_table[first + place], rows, :] for place in range(2)]
        return jnp.concatenate(pieces, axis=1)

    query_rows, value_rows = pl.ds(0, HD), pl.ds(HD, HD)
    queries = joined(turned_ref, 2 * tile, query_rows)

    def step(state, keys, values, visible):
        largest, weight_sum = state
        scores = jnp.dot(keys, queries, preferred_element_type=jnp.float32)
        if visible is not None:
            scores = jnp.where(visible, scores, lowest)
        new_largest = jnp.maximum(largest, jnp.max(scores, axis=0, keepdims=True))
        weights = jnp.exp2((scores - new_largest) * factor)
        fade = jnp.exp2((largest - new_largest) * factor)
        weight_sum = weight_sum * fade + jnp.sum(weights, axis=0, keepdims=True)
        total_ref[...] = total_ref[...] * fade + jnp.dot(
            values, weights.astype(jnp.bfloat16), preferred_element_type=jnp.float32
        )
        return (new_largest, weight_sum)

    def new_step(number, state, visible=None):
        first = 2 * number
        pieces = [keys_ref[chunk_table[first + place]] for place in range(2)]
        keys = jnp.concatenate(pieces, axis=0)
        return step(state, keys, joined(turned_ref, first, value_rows), visible)

    def cache_step(number, state):
        place = pl.ds(pl.multiple_of(number * CHUNK, CHUNK), CHUNK)
        row = lax.broadcasted_iota(jnp.int32, (CHUNK, width), 0)
        visible = row + number * CHUNK < length
        return step(state, cached_keys[place, :], cached_values[:, place], visible)

    total_ref[...] = jnp.zeros_like(total_ref)
    state = (jnp.full((1, width), lowest, jnp.float32), jnp.zeros((1, width), jnp.float32))
    key_row = lax.broadcasted_iota(jnp.int32, (width, width), 0)
    query_column = lax.broadcasted_iota(jnp.int32, (width, width), 1)
    state = new_step(tile, state, key_row <= query_column)
    state = lax.fori_loop(0, tile, new_step, state)
    state = lax.fori_loop(0, pl.cdiv(length, CHUNK), cache_step, state)
    out_ref[...] = (total_ref[...] / state[1]).astype(jnp.bfloat16)


def attention(half, turned, keys, cache_blocks, chunk_table, cache_table, length):
    whole = lambda array: pl.BlockSpec(array.shape, lambda i, *_: (0, 0, 0))
    cache_span = cache_table.shape[0] * CHUNK
    return pl.pallas_call(
        functools.partial(attention_kernel, half),
        grid_spec=pltpu.PrefetchScalarGridSpec(
            num_scalar_prefetch=3,
            grid=(QLEN // (4 * CHUNK),),
            in_specs=[whole(array) for array in (turned, keys, *cache_blocks)],
            out_specs=pl.BlockSpec((HD, 2 * CHUNK), lambda i, *_: (0, i)),
            scratch_shapes=[
                pltpu.VMEM((HD, 2 * CHUNK), jnp.float32),
                pltpu.VMEM((cache_span, HD), jnp.bfloat16),
                pltpu.VMEM((HD, cache_span), jnp.bfloat16),
            ],
        ),
        out_shape=jax.ShapeDtypeStruct((HD, QLEN // 2), jnp.bfloat16),
        compiler_params=pltpu.CompilerParams(vmem_limit_bytes=48 * 2**20),
        cost_estimate=pl.CostEstimate(flops=1, bytes_accessed=1, transcendentals=0),
    )(chunk_table, cache_table, length, turned, keys, *cache_blocks)


def per_device_paired(
    inputs,
    norm_gain,
    qkv_weight,
    adapter_down,
    adapter_up,
    out_weight,
    cache_keys,
    cache_values,
    cache_lengths,
    block_perm,
):
    tok_dev, width = inputs.shape
    rows = qkv_weight.shape[0]
    plane, side = lax.axis_index("z"), lax.axis_index("x")
    row, core = lax.axis_index("y"), lax.axis_index("core")
    seq, mp = 2 * plane + side, 2 * row + core
    role = plane % 2

    def over_z(array, bit):
        return swap(array, "z", 4, bit)

    def over_x(array):
        return swap(array, "x", 2, 1)

    def over_y(array):
        return swap(array, "y", 2, 1)

    def over_core(array):
        return swap(array, "core", 2, 1)

    part = normalise(inputs, norm_gain, mp, CHUNK)
    plane_axes = ("x", "y", "core")
    plane_axes = ("x", "y", "core")
    part_z = over_z(part, 1)
    part_x = over_x(part)

    turned = qkv_weight.reshape(rows, 3, 4, HD).transpose(2, 1, 3, 0).reshape(2, 2, 3 * HD, rows)
    kept = pick(turned, side, 1)
    given = pick(turned, 1 - side, 1)
    from_x = over_x(jnp.stack([pick(given, role), pick(given, 1 - role)]))
    kept_near = pick(kept, 1 - role)
    far = {bit: [over_z(pick(kept, role ^ (bit & 1)), bit)] for bit in (2, 3)}
    share = lax.dynamic_slice_in_dim(adapter_down, mp * (rows // 4), rows // 4, 0)
    down = lax.all_gather(share, ("z", "x", "y", "core"), axis=0, tiled=True)

    def turned_cache(cache):
        blocks, size, _ = cache.shape
        return cache.reshape(blocks * size, 4, HD).transpose(1, 2, 0)

    cached = jnp.concatenate([turned_cache(cache_keys), turned_cache(cache_values)], axis=1)
    cached = cached.reshape(2, 2, 2 * HD, cached.shape[2])

    part_z, part_x, from_x, far[2][0], far[3][0], kept_near, cached, down, inputs = fence(
        part_z, part_x, from_x, far[2][0], far[3][0], kept_near, cached, down, inputs
    )
    pair_tokens = lax.all_gather(part_z, plane_axes, axis=0, tiled=True)
    near = over_z(jnp.stack([kept_near, from_x[1]]), 1)
    for bit in (2, 3):
        far[bit].append(over_z(from_x[bit & 1], bit))
    cache_from_x = over_x(pick(cached, 1 - side, 1))
    part_y = over_y(part_x[:GROUP])
    normed = normalise(inputs, norm_gain, jnp.int32(0), tok_dev)
    down = down.T

    near, far[2][1], far[3][1], cache_from_x, part_y, normed, part_x, down, cached = fence(
        near, far[2][1], far[3][1], cache_from_x, part_y, normed, part_x, down, cached
    )
    cache_both = jnp.stack([pick(cached, side, 1), cache_from_x], axis=1)
    cache_blocks = [pick(cache_both, role)]
    for bit in (1, 2, 3):
        cache_blocks.append(over_z(pick(cache_both, role ^ (bit & 1)), bit))
    core_x = over_core(part_x)
    start = (mp ^ 2) * CHUNK + GROUP
    part_yx = over_x(lax.dynamic_slice_in_dim(normed, start, GROUP, 0))
    weight_blocks = [pick(kept, role), from_x[0], near[0], near[1], *far[2], *far[3]]
    order = jnp.arange(8, dtype=jnp.int32) ^ seq
    up = adapter_up.reshape(3, RANK, 4, HD).transpose(2, 0, 3, 1).reshape(4, 3 * HD, RANK)
    up = pick(up, 2 * role + side)

    requests = jnp.stack([plane, plane ^ 1])
    lengths = lookup(cache_lengths, requests)
    logical = requests[:, None] * 4 + jnp.arange(4, dtype=jnp.int32)[None, :]
    hits = logical[..., None] == block_perm
    physical = jnp.sum(
        jnp.where(hits, jnp.arange(block_perm.shape[0], dtype=jnp.int32), 0), axis=-1
    )
    cache_table = (((physical // 2) ^ seq) * 2 + physical % 2).astype(jnp.int32)

    def attend(number, half, projected):
        turned_rows, key_rows = projected
        return attention(
            half,
            turned_rows,
            key_rows,
            cache_blocks,
            chunk_tables[number],
            cache_table[number],
            lengths[number : number + 1],
        )

    half_dev = tok_dev // 2

    place = jnp.arange(8, dtype=jnp.int32)
    moved = (place % 4) ^ mp
    chunk_tables = (
        jnp.where(place // 4 == side, place % 4, 4 + moved),
        place,
    )
    local_projected = project((normed,), up, down, weight_blocks, order)

    *cache_blocks, up, local_turned, local_keys, out_weight, core_x, part_y, part_yx = fence(
        *cache_blocks, up, *local_projected, out_weight, core_x, part_y, part_yx
    )
    pair_projected = project((pair_tokens,), up, down, weight_blocks, order)
    pair_first = attend(1, 0, pair_projected)
    part_y, part_yx = fence(part_y, part_yx, pair_projected[0])[:2]
    part_y = jnp.concatenate([part_y, part_yx])
    core_y = over_core(part_y)
    pair_first, core_y, part_y, up, pair_turned = fence(
        pair_first, core_y, part_y, up, pair_projected[0]
    )

    out_rows = lax.all_gather(out_weight, ("z", "x"), axis=1, tiled=True)
    out_cols = out_rows.shape[1] // 4

    def out_columns(to_row, to_core):
        return lax.dynamic_slice_in_dim(out_rows, (2 * to_row + to_core) * out_cols, out_cols, 1)

    columns = {
        "away_core": out_columns(1 - row, 1 - core),
        "away": out_columns(1 - row, core),
        "here_core": out_columns(row, 1 - core),
        "here": out_columns(row, core),
    }

    def rounded(array):
        return array.astype(jnp.bfloat16)

    def out_part(heads, name):
        return lax.dot_general(
            heads, columns[name], (((0,), (0,)), ((), ())), preferred_element_type=jnp.float32
        )

    def crossing(attended):
        return lax.dynamic_slice_in_dim(attended, (1 - side) * half_dev, half_dev, 1)

    def both_sides(attended, theirs):
        mine = lax.dynamic_slice_in_dim(attended, side * half_dev, half_dev, 1)
        return jnp.where(side == 0, jnp.stack([mine, theirs]), jnp.stack([theirs, mine]))

    def all_heads(own, own_theirs, pair, pair_theirs):
        own_heads, pair_heads = both_sides(own, own_theirs), both_sides(pair, pair_theirs)
        return jnp.where(
            role == 0,
            jnp.concatenate([own_heads, pair_heads]),
            jnp.concatenate([pair_heads, own_heads]),
        ).reshape(4 * HD, half_dev)

    def summed(heads):
        away = over_core(rounded(out_part(heads, "away_core")))
        here = over_core(rounded(out_part(heads, "here_core")))
        away = rounded(out_part(heads, "away") + away.astype(jnp.float32))
        return away, out_part(heads, "here") + here.astype(jnp.float32)

    pair_first = over_z(pair_first, 1)
    parts_projected = project((part_x, core_x, part_y, core_y), up, down, weight_blocks, order)
    pair_first, parts_turned, parts_keys = fence(pair_first, *parts_projected)
    pair_first_crossed = over_x(crossing(pair_first))
    own_projected = (
        jnp.concatenate([local_turned, parts_turned]),
        jnp.concatenate([local_keys, parts_keys]),
    )
    own_first = attend(0, 0, own_projected)
    pair_first_crossed, own_first, pair_turned, own_turned = fence(
        pair_first_crossed, own_first, pair_turned, own_projected[0]
    )
    own_first_crossed = over_x(crossing(own_first))
    pair_second = attend(1, 1, (pair_turned, pair_projected[1]))
    own_first_crossed, pair_second = fence(own_first_crossed, pair_second)
    pair_second = over_z(pair_second, 1)
    first_sent, first_here = summed(
        all_heads(own_first, own_first_crossed, pair_first, pair_first_crossed)
    )
    pair_second, first_sent, first_here, own_turned = fence(
        pair_second, first_sent, first_here, own_turned
    )
    first_received = over_y(first_sent)
    pair_second_crossed = over_x(crossing(pair_second))
    own_second = attend(0, 1, (own_turned, own_projected[1]))
    pair_second_crossed, own_second = fence(pair_second_crossed, own_second)
    own_second_crossed = over_x(crossing(own_second))
    own_second_crossed, first_received = fence(own_second_crossed, first_received)
    second_sent, second_here = summed(
        all_heads(own_second, own_second_crossed, pair_second, pair_second_crossed)
    )
    second_received = over_y(second_sent)
    return jnp.concatenate(
        [
            rounded(first_here + first_received.astype(jnp.float32)),
            rounded(second_here + second_received.astype(jnp.float32)),
        ]
    )


def solution(mesh):
    paired = mesh.shape["seq"] == 8 and mesh.shape["mp"] == 4
    if paired:
        seq, mp = ("z", "x"), ("y", "core")
        mesh = jax.sharding.Mesh(mesh.devices.reshape(4, 2, 2, 2), seq + mp)
    else:
        seq, mp = "seq", "mp"
    in_specs = (
        P(seq, None),
        P(),
        P(seq, None, mp),
        P(seq, None),
        P(None, None, mp),
        P(mp, seq),
        P(seq, None, mp),
        P(seq, None, mp),
        P(),
        P(),
    )
    return jax.shard_map(
        per_device_paired if paired else per_device,
        mesh=mesh,
        in_specs=in_specs,
        out_specs=P(seq, mp),
        check_vma=False,
    )
```

```python
import functools

import jax
import jax.numpy as jnp
from jax import lax
from jax.experimental import pallas as pl
from jax.experimental.pallas import tpu as pltpu
from jax.sharding import PartitionSpec as P

HD = 224
REQS = 4
QLEN = 2048


lowest = -1e30


def lookup(small_table, positions_of):
    hits = positions_of[..., None] == jnp.arange(small_table.shape[0], dtype=jnp.int32)
    return jnp.sum(jnp.where(hits, small_table, 0), axis=-1)


def query_meta(token_index, lengths):
    request = token_index // QLEN
    return (request, lookup(lengths, request) + token_index % QLEN)


def key_meta(row_index, layout, permutation, lengths):
    cache_rows, block_size, tok_dev, max_blocks = layout
    rows_dev = cache_rows + tok_dev
    device = row_index // rows_dev
    local_row = row_index % rows_dev
    block_index = (
        device * (cache_rows // block_size) + jnp.minimum(local_row, cache_rows - 1) // block_size
    )
    logical = lookup(permutation, block_index)
    request = logical // max_blocks
    position = logical % max_blocks * block_size + local_row % block_size
    cached_live = position < lookup(lengths, request)
    new_req, new_pos = query_meta(device * tok_dev + local_row - cache_rows, lengths)
    in_cache = local_row < cache_rows
    key_req = jnp.where(in_cache, jnp.where(cached_live, request, -1), new_req)
    return (key_req, jnp.where(in_cache, position, new_pos))


def attend(softmax_state, queries, query_info, key_rows, value_rows, key_info, head_dim):
    query_req, query_pos = query_info
    key_req, key_pos = key_info
    visible = (key_req[None, :] == query_req[:, None]) & (key_pos[None, :] <= query_pos[:, None])
    query_count = queries.shape[0]
    key_count = key_rows.shape[0]
    head_count = queries.shape[1] // head_dim
    summed, largest, weight_sum = softmax_state
    scores = jnp.einsum(
        "qhd,khd->hqk",
        queries.reshape(query_count, head_count, head_dim),
        key_rows.reshape(key_count, head_count, head_dim),
        preferred_element_type=jnp.float32,
    ) * head_dim ** (-0.5)
    scores = jnp.where(visible[None], scores, lowest)
    new_largest = jnp.maximum(largest, jnp.max(scores, axis=-1))
    weights = jnp.where(visible[None], jnp.exp(scores - new_largest[..., None]), 0.0)
    weight_sum = jnp.sum(weights, axis=-1)
    summed = jnp.einsum(
        "hqk,khd->hqd",
        weights.astype(jnp.bfloat16),
        value_rows.reshape(key_count, head_count, head_dim),
        preferred_element_type=jnp.float32,
    )
    return (summed, new_largest, weight_sum)


def per_device(
    inputs,
    norm_gain,
    qkv_weight,
    adapter_down,
    adapter_up,
    out_weight,
    cache_keys,
    cache_values,
    cache_lengths,
    block_perm,
):
    tok_dev = inputs.shape[0]
    widened = inputs.astype(jnp.float32)
    normed = (
        widened * lax.rsqrt(jnp.mean(widened * widened, axis=-1, keepdims=True) + 1e-05) * norm_gain
    ).astype(jnp.bfloat16)
    head_width = qkv_weight.shape[2]
    weight_rows = lax.all_gather(qkv_weight, "seq", axis=0, tiled=True)
    down_rows = lax.all_gather(adapter_down, "seq", axis=0, tiled=True)
    main_part = jnp.einsum("tr,rkc->ktc", normed, weight_rows, preferred_element_type=jnp.float32)
    low_rank = jnp.dot(normed, down_rows, preferred_element_type=jnp.float32)
    main_part, low_rank = (main_part, low_rank)
    low_rank = low_rank.astype(jnp.bfloat16)
    projected = (
        main_part
        + jnp.einsum("tr,krc->ktc", low_rank, adapter_up, preferred_element_type=jnp.float32)
    ).astype(jnp.bfloat16)
    queries = projected[0]
    new_keys = projected[1]
    new_values = projected[2]
    cycle_index = lax.axis_index("seq")
    cache_rows = cache_keys.shape[0] * cache_keys.shape[1]
    layout = (cache_rows, cache_keys.shape[1], tok_dev, block_perm.shape[0] // REQS)
    key_rows = jnp.concatenate([cache_keys.reshape(cache_rows, head_width), new_keys], axis=0)
    value_rows = jnp.concatenate([cache_values.reshape(cache_rows, head_width), new_values], axis=0)
    token_ids = jnp.arange(tok_dev, dtype=jnp.int32)
    own_info = query_meta(cycle_index * tok_dev + token_ids, cache_lengths)
    head_count = head_width // HD
    softmax_state = (
        jnp.zeros((head_count, tok_dev, HD), jnp.float32),
        jnp.full((head_count, tok_dev), lowest, jnp.float32),
        jnp.zeros((head_count, tok_dev), jnp.float32),
    )
    pieces = (
        lax.all_gather(key_rows, "seq", axis=0, tiled=True),
        lax.all_gather(value_rows, "seq", axis=0, tiled=True),
    )
    row_ids = jnp.arange(pieces[0].shape[0], dtype=jnp.int32)
    key_info = key_meta(row_ids, layout, block_perm, cache_lengths)
    softmax_state = attend(softmax_state, queries, own_info, pieces[0], pieces[1], key_info, HD)
    summed, largest, weight_sum = softmax_state
    attended = (
        (summed / weight_sum[..., None])
        .transpose(1, 0, 2)
        .reshape(tok_dev, head_width)
        .astype(jnp.bfloat16)
    )
    partial_value = jnp.dot(
        attended,
        lax.all_gather(out_weight, "seq", axis=1, tiled=True),
        preferred_element_type=jnp.float32,
    )
    return lax.psum_scatter(
        partial_value.astype(jnp.bfloat16), "mp", scatter_dimension=1, tiled=True
    )


CHUNK = 256
GROUP = 128
RANK = 128
LOG2E = 1.4426950408889634


def swap(array, axis, size, bit):
    return lax.ppermute(array, axis, [(i, i ^ bit) for i in range(size)])


def pick(array, index, axis=0):
    return lax.dynamic_index_in_dim(array, index, axis, keepdims=False)


def after(array, *earlier):
    return lax.optimization_barrier((array, *earlier))[0]


def fence(*arrays):
    return lax.optimization_barrier(arrays)


def norm_kernel(first, inputs_ref, gain_ref, out_ref):
    widened = inputs_ref[...].astype(jnp.float32)
    mean = jnp.mean(widened * widened, axis=-1, keepdims=True)
    out_ref[...] = (widened * lax.rsqrt(mean + 1e-05) * gain_ref[...]).astype(jnp.bfloat16)


def normalise(inputs, norm_gain, part, count):
    width = inputs.shape[1]
    rows = 64
    steps = count // rows
    return pl.pallas_call(
        norm_kernel,
        grid_spec=pltpu.PrefetchScalarGridSpec(
            num_scalar_prefetch=1,
            grid=(steps,),
            in_specs=[
                pl.BlockSpec((rows, width), lambda i, first: (first[0] * steps + i, 0)),
                pl.BlockSpec((1, width), lambda i, first: (0, 0)),
            ],
            out_specs=pl.BlockSpec((rows, width), lambda i, first: (i, 0)),
        ),
        out_shape=jax.ShapeDtypeStruct((count, width), jnp.bfloat16),
        compiler_params=pltpu.CompilerParams(vmem_limit_bytes=40 * 2**20),
        cost_estimate=pl.CostEstimate(flops=1, bytes_accessed=1, transcendentals=0),
    )(part.reshape(1), inputs, norm_gain.reshape(1, width))


def project_kernel(sets, order, up_ref, down_ref, *refs):
    token_refs, weight_refs = refs[: len(sets)], refs[len(sets) : -3]
    turned_ref, keys_ref, held_ref = refs[-3:]
    rows = weight_refs[0].shape[1]
    main = 3 * HD
    step = pl.program_id(0)

    @pl.when(step == 0)
    def fill():
        for number, weight_ref in enumerate(weight_refs):
            columns = pl.ds(pl.multiple_of(order[number] * rows, 128), rows)
            held_ref[pl.ds(0, main), columns] = weight_ref[...]
        held_ref[pl.ds(main, RANK), :] = down_ref[...]

    def run(tokens_ref):
        total = lax.dot_general(
            held_ref[...],
            tokens_ref[...],
            (((1,), (1,)), ((), ())),
            preferred_element_type=jnp.float32,
        )
        low_rank = total[main:].astype(jnp.bfloat16)
        total = total[:main] + jnp.dot(up_ref[...], low_rank, preferred_element_type=jnp.float32)
        for number in range(turned_ref.shape[0]):
            columns = slice(number * CHUNK, (number + 1) * CHUNK)
            turned_ref[number, pl.ds(0, HD), :] = total[:HD, columns].astype(jnp.bfloat16)
            turned_ref[number, pl.ds(HD, HD), :] = total[2 * HD :, columns].astype(jnp.bfloat16)
            keys_ref[number] = total[HD : 2 * HD, columns].T.astype(jnp.bfloat16)

    for (first, count), tokens_ref in zip(sets, token_refs):
        pl.when((step >= first) & (step < first + count))(functools.partial(run, tokens_ref))


def project(token_sets, up, down, weight_blocks, order):
    width = token_sets[0].shape[1]
    per_step = 1 if len(token_sets) > 1 else 2
    main = 3 * HD
    sets, steps = [], 0
    for tokens in token_sets:
        sets.append((steps, tokens.shape[0] // (per_step * CHUNK)))
        steps += sets[-1][1]
    chunks = steps * per_step
    whole = lambda array: pl.BlockSpec(array.shape, lambda i, *_: (0,) * array.ndim)

    def token_spec(first, count):
        return pl.BlockSpec(
            (per_step * CHUNK, width), lambda i, *_: (jnp.clip(i - first, 0, count - 1), 0)
        )

    return pl.pallas_call(
        functools.partial(project_kernel, tuple(sets)),
        grid_spec=pltpu.PrefetchScalarGridSpec(
            num_scalar_prefetch=1,
            grid=(steps,),
            in_specs=[whole(array) for array in (up, down)]
            + [token_spec(*one) for one in sets]
            + [
                pl.BlockSpec(
                    (main, array.shape[1]), lambda i, *_: (0, 0), pipeline_mode=pl.Buffered(1)
                )
                for array in weight_blocks
            ],
            out_specs=[
                pl.BlockSpec((per_step, 2 * HD, CHUNK), lambda i, *_: (i, 0, 0)),
                pl.BlockSpec((per_step, CHUNK, HD), lambda i, *_: (i, 0, 0)),
            ],
            scratch_shapes=[pltpu.VMEM((main + RANK, width), jnp.bfloat16)],
        ),
        out_shape=[
            jax.ShapeDtypeStruct((chunks, 2 * HD, CHUNK), jnp.bfloat16),
            jax.ShapeDtypeStruct((chunks, CHUNK, HD), jnp.bfloat16),
        ],
        compiler_params=pltpu.CompilerParams(vmem_limit_bytes=58 * 2**20),
        cost_estimate=pl.CostEstimate(flops=1, bytes_accessed=1, transcendentals=0),
    )(order, up, down, *token_sets, *weight_blocks)


def attention_kernel(
    half,
    chunk_table,
    cache_table,
    length_ref,
    turned_ref,
    keys_ref,
    *refs,
):
    block_refs, (out_ref, total_ref, cached_keys, cached_values) = refs[:-4], refs[-4:]
    tile = 2 * pl.program_id(0) + half
    factor = HD ** (-0.5) * LOG2E
    width = 2 * CHUNK
    length = length_ref[0]

    @pl.when(pl.program_id(0) == 0)
    def gather_cache():
        for number in range(cache_table.shape[0]):
            entry = cache_table[number]

            @pl.when(number * CHUNK >= length)
            def clear(number=number):
                place = pl.ds(number * CHUNK, CHUNK)
                cached_values[:, place] = jnp.zeros((HD, CHUNK), jnp.bfloat16)

            for bit, block_ref in enumerate(block_refs):

                @pl.when((number * CHUNK < length) & (entry // 4 == bit))
                def take(number=number, entry=entry, block_ref=block_ref):
                    other = (entry // 2) % 2
                    columns = pl.ds(pl.multiple_of((entry % 2) * CHUNK, CHUNK), CHUNK)
                    place = pl.ds(number * CHUNK, CHUNK)
                    keys = block_ref[other, pl.ds(0, HD), columns].astype(jnp.float32)
                    cached_keys[place, :] = keys.T.astype(jnp.bfloat16)
                    cached_values[:, place] = block_ref[other, pl.ds(HD, HD), columns]

    def joined(ref, first, rows):
        pieces = [ref[chunk_table[first + place], rows, :] for place in range(2)]
        return jnp.concatenate(pieces, axis=1)

    query_rows, value_rows = pl.ds(0, HD), pl.ds(HD, HD)
    queries = joined(turned_ref, 2 * tile, query_rows)

    def step(state, keys, values, visible):
        largest, weight_sum = state
        scores = jnp.dot(keys, queries, preferred_element_type=jnp.float32)
        if visible is not None:
            scores = jnp.where(visible, scores, lowest)
        new_largest = jnp.maximum(largest, jnp.max(scores, axis=0, keepdims=True))
        weights = jnp.exp2((scores - new_largest) * factor)
        fade = jnp.exp2((largest - new_largest) * factor)
        weight_sum = weight_sum * fade + jnp.sum(weights, axis=0, keepdims=True)
        total_ref[...] = total_ref[...] * fade + jnp.dot(
            values, weights.astype(jnp.bfloat16), preferred_element_type=jnp.float32
        )
        return (new_largest, weight_sum)

    def new_step(number, state, visible=None):
        first = 2 * number
        pieces = [keys_ref[chunk_table[first + place]] for place in range(2)]
        keys = jnp.concatenate(pieces, axis=0)
        return step(state, keys, joined(turned_ref, first, value_rows), visible)

    def cache_step(number, state):
        place = pl.ds(pl.multiple_of(number * width, width), width)
        visible = key_row + number * width < length
        return step(state, cached_keys[place, :], cached_values[:, place], visible)

    total_ref[...] = jnp.zeros_like(total_ref)
    state = (jnp.full((1, width), lowest, jnp.float32), jnp.zeros((1, width), jnp.float32))
    key_row = lax.broadcasted_iota(jnp.int32, (width, width), 0)
    query_column = lax.broadcasted_iota(jnp.int32, (width, width), 1)
    state = new_step(tile, state, key_row <= query_column)
    state = lax.fori_loop(0, tile, new_step, state)
    state = lax.fori_loop(0, pl.cdiv(length, width), cache_step, state)
    out_ref[...] = (total_ref[...] / state[1]).astype(jnp.bfloat16)


def attention(half, turned, keys, cache_blocks, chunk_table, cache_table, length):
    whole = lambda array: pl.BlockSpec(array.shape, lambda i, *_: (0, 0, 0))
    cache_span = cache_table.shape[0] * CHUNK
    return pl.pallas_call(
        functools.partial(attention_kernel, half),
        grid_spec=pltpu.PrefetchScalarGridSpec(
            num_scalar_prefetch=3,
            grid=(QLEN // (4 * CHUNK),),
            in_specs=[whole(array) for array in (turned, keys, *cache_blocks)],
            out_specs=pl.BlockSpec((HD, 2 * CHUNK), lambda i, *_: (0, i)),
            scratch_shapes=[
                pltpu.VMEM((HD, 2 * CHUNK), jnp.float32),
                pltpu.VMEM((cache_span, HD), jnp.bfloat16),
                pltpu.VMEM((HD, cache_span), jnp.bfloat16),
            ],
        ),
        out_shape=jax.ShapeDtypeStruct((HD, QLEN // 2), jnp.bfloat16),
        compiler_params=pltpu.CompilerParams(vmem_limit_bytes=48 * 2**20),
        cost_estimate=pl.CostEstimate(flops=1, bytes_accessed=1, transcendentals=0),
    )(chunk_table, cache_table, length, turned, keys, *cache_blocks)


def per_device_paired(
    inputs,
    norm_gain,
    qkv_weight,
    adapter_down,
    adapter_up,
    out_weight,
    cache_keys,
    cache_values,
    cache_lengths,
    block_perm,
):
    tok_dev, width = inputs.shape
    rows = qkv_weight.shape[0]
    plane, side = lax.axis_index("z"), lax.axis_index("x")
    row, core = lax.axis_index("y"), lax.axis_index("core")
    seq, mp = 2 * plane + side, 2 * row + core
    role = plane % 2

    def over_z(array, bit):
        return swap(array, "z", 4, bit)

    def over_x(array):
        return swap(array, "x", 2, 1)

    def over_y(array):
        return swap(array, "y", 2, 1)

    def over_core(array):
        return swap(array, "core", 2, 1)

    part = normalise(inputs, norm_gain, mp, CHUNK)
    plane_axes = ("x", "y", "core")
    plane_axes = ("x", "y", "core")
    part_z = over_z(part, 1)
    part_x = over_x(part)

    turned = qkv_weight.reshape(rows, 3, 4, HD).transpose(2, 1, 3, 0).reshape(2, 2, 3 * HD, rows)
    kept = pick(turned, side, 1)
    given = pick(turned, 1 - side, 1)
    from_x = over_x(jnp.stack([pick(given, role), pick(given, 1 - role)]))
    kept_near = pick(kept, 1 - role)
    far = {bit: [over_z(pick(kept, role ^ (bit & 1)), bit)] for bit in (2, 3)}
    share = lax.dynamic_slice_in_dim(adapter_down, mp * (rows // 4), rows // 4, 0)
    down = lax.all_gather(share, ("z", "x", "y", "core"), axis=0, tiled=True)

    def turned_cache(cache):
        blocks, size, _ = cache.shape
        return cache.reshape(blocks * size, 4, HD).transpose(1, 2, 0)

    cached = jnp.concatenate([turned_cache(cache_keys), turned_cache(cache_values)], axis=1)
    cached = cached.reshape(2, 2, 2 * HD, cached.shape[2])

    near_rows = jnp.stack([kept_near, from_x[1]])
    same_rows, other_rows = from_x[0], from_x[1]
    cache_own, cache_given = pick(cached, side, 1), pick(cached, 1 - side, 1)
    (
        part_z,
        part_x,
        near_rows,
        same_rows,
        other_rows,
        far[2][0],
        far[3][0],
        cache_own,
        cache_given,
        down,
        inputs,
    ) = fence(
        part_z,
        part_x,
        near_rows,
        same_rows,
        other_rows,
        far[2][0],
        far[3][0],
        cache_own,
        cache_given,
        down,
        inputs,
    )
    pair_tokens = lax.all_gather(part_z, plane_axes, axis=0, tiled=True)
    near = over_z(near_rows, 1)
    far[2].append(over_z(same_rows, 2))
    far[3].append(over_z(other_rows, 3))
    cache_from_x = over_x(cache_given)
    core_x = over_core(part_x)
    normed = normalise(inputs, norm_gain, jnp.int32(0), tok_dev)
    down = down.T

    start = (mp ^ 2) * CHUNK + GROUP
    given_x = lax.dynamic_slice_in_dim(normed, start, GROUP, 0)
    given_y = part_x[:GROUP]
    cache_both = jnp.stack([cache_own, cache_from_x], axis=1)
    cache_same, cache_other = pick(cache_both, role), pick(cache_both, 1 - role)
    near, far[2][1], far[3][1], cache_same, cache_other, core_x, normed, part_x = fence(
        near, far[2][1], far[3][1], cache_same, cache_other, core_x, normed, part_x
    )
    given_x, given_y, down, part_x = fence(given_x, given_y, down, part_x)
    cache_blocks = [
        cache_same,
        over_z(cache_other, 1),
        over_z(cache_same, 2),
        over_z(cache_other, 3),
    ]
    part_y = over_y(given_y)
    part_yx = over_x(given_x)
    weight_blocks = [pick(kept, role), same_rows, near[0], near[1], *far[2], *far[3]]
    order = jnp.arange(8, dtype=jnp.int32) ^ seq
    up = adapter_up.reshape(3, RANK, 4, HD).transpose(2, 0, 3, 1).reshape(4, 3 * HD, RANK)
    up = pick(up, 2 * role + side)

    requests = jnp.stack([plane, plane ^ 1])
    lengths = lookup(cache_lengths, requests)
    logical = requests[:, None] * 4 + jnp.arange(4, dtype=jnp.int32)[None, :]
    hits = logical[..., None] == block_perm
    physical = jnp.sum(
        jnp.where(hits, jnp.arange(block_perm.shape[0], dtype=jnp.int32), 0), axis=-1
    )
    cache_table = (((physical // 2) ^ seq) * 2 + physical % 2).astype(jnp.int32)

    def attend(number, half, projected):
        turned_rows, key_rows = projected
        return attention(
            half,
            turned_rows,
            key_rows,
            cache_blocks,
            chunk_tables[number],
            cache_table[number],
            lengths[number : number + 1],
        )

    half_dev = tok_dev // 2

    place = jnp.arange(8, dtype=jnp.int32)
    moved = (place % 4) ^ mp
    chunk_tables = (
        jnp.where(place // 4 == side, place % 4, 4 + moved),
        place,
    )
    local_projected = project((normed, part_x, core_x), up, down, weight_blocks, order)

    *cache_blocks, up, local_turned, local_keys, out_weight, part_y, part_yx = fence(
        *cache_blocks, up, *local_projected, out_weight, part_y, part_yx
    )
    part_y = jnp.concatenate([part_y, part_yx])
    core_y = over_core(part_y)
    pair_projected = project((pair_tokens,), up, down, weight_blocks, order)
    pair_first = attend(1, 0, pair_projected)
    pair_first, pair_turned, core_y, up = fence(pair_first, pair_projected[0], core_y, up)

    out_rows = lax.all_gather(out_weight, ("z", "x"), axis=1, tiled=True)
    out_cols = out_rows.shape[1] // 4

    def out_columns(to_row, to_core):
        return lax.dynamic_slice_in_dim(out_rows, (2 * to_row + to_core) * out_cols, out_cols, 1)

    columns = {
        "away_core": out_columns(1 - row, 1 - core),
        "away": out_columns(1 - row, core),
        "here_core": out_columns(row, 1 - core),
        "here": out_columns(row, core),
    }

    def rounded(array):
        return array.astype(jnp.bfloat16)

    def out_part(heads, name):
        return lax.dot_general(
            heads, columns[name], (((0,), (0,)), ((), ())), preferred_element_type=jnp.float32
        )

    def summed(heads):
        away = over_core(rounded(out_part(heads, "away_core")))
        here = over_core(rounded(out_part(heads, "here_core")))
        away = rounded(out_part(heads, "away") + away.astype(jnp.float32))
        return away, out_part(heads, "here") + here.astype(jnp.float32)

    def crossing(attended):
        return lax.dynamic_slice_in_dim(attended, (1 - side) * half_dev, half_dev, 1)

    def both_sides(attended, theirs):
        mine = lax.dynamic_slice_in_dim(attended, side * half_dev, half_dev, 1)
        return jnp.where(side == 0, jnp.stack([mine, theirs]), jnp.stack([theirs, mine]))

    def all_heads(own, own_theirs, pair, pair_theirs):
        own_heads, pair_heads = both_sides(own, own_theirs), both_sides(pair, pair_theirs)
        return jnp.where(
            role == 0,
            jnp.concatenate([own_heads, pair_heads]),
            jnp.concatenate([pair_heads, own_heads]),
        ).reshape(4 * HD, half_dev)

    pair_first = over_z(pair_first, 1)
    parts_turned, parts_keys = project((part_y, core_y), up, down, weight_blocks, order)
    own_keys = jnp.concatenate([local_keys, parts_keys])
    own_turned = jnp.concatenate([local_turned, parts_turned])
    pair_first, own_turned, own_keys = fence(pair_first, own_turned, own_keys)
    pair_first_crossed = over_x(crossing(pair_first))
    own_first = attend(0, 0, (own_turned, own_keys))
    pair_first_crossed, own_first, pair_turned, own_turned = fence(
        pair_first_crossed, own_first, pair_turned, own_turned
    )
    own_first_crossed = over_x(crossing(own_first))
    pair_second = attend(1, 1, (pair_turned, pair_projected[1]))
    own_first_crossed, pair_second = fence(own_first_crossed, pair_second)
    pair_second = over_z(pair_second, 1)
    first_sent, first_here = summed(
        all_heads(own_first, own_first_crossed, pair_first, pair_first_crossed)
    )
    pair_second, first_sent, first_here, own_turned = fence(
        pair_second, first_sent, first_here, own_turned
    )
    first_received = over_y(first_sent)
    pair_second_crossed = over_x(crossing(pair_second))
    own_second = attend(0, 1, (own_turned, own_keys))
    pair_second_crossed, own_second = fence(pair_second_crossed, own_second)
    own_second_crossed = over_x(crossing(own_second))
    own_second_crossed, first_received = fence(own_second_crossed, first_received)
    second_sent, second_here = summed(
        all_heads(own_second, own_second_crossed, pair_second, pair_second_crossed)
    )
    second_received = over_y(second_sent)
    return jnp.concatenate(
        [
            rounded(first_here + first_received.astype(jnp.float32)),
            rounded(second_here + second_received.astype(jnp.float32)),
        ]
    )


def solution(mesh):
    paired = mesh.shape["seq"] == 8 and mesh.shape["mp"] == 4
    if paired:
        seq, mp = ("z", "x"), ("y", "core")
        mesh = jax.sharding.Mesh(mesh.devices.reshape(4, 2, 2, 2), seq + mp)
    else:
        seq, mp = "seq", "mp"
    in_specs = (
        P(seq, None),
        P(),
        P(seq, None, mp),
        P(seq, None),
        P(None, None, mp),
        P(mp, seq),
        P(seq, None, mp),
        P(seq, None, mp),
        P(),
        P(),
    )
    return jax.shard_map(
        per_device_paired if paired else per_device,
        mesh=mesh,
        in_specs=in_specs,
        out_specs=P(seq, mp),
        check_vma=False,
    )
```

```python
import functools

import jax
import jax.numpy as jnp
from jax import lax
from jax.experimental import pallas as pl
from jax.experimental.pallas import tpu as pltpu
from jax.sharding import PartitionSpec as P

HD = 224
REQS = 4
QLEN = 2048


lowest = -1e30


def lookup(small_table, positions_of):
    hits = positions_of[..., None] == jnp.arange(small_table.shape[0], dtype=jnp.int32)
    return jnp.sum(jnp.where(hits, small_table, 0), axis=-1)


def query_meta(token_index, lengths):
    request = token_index // QLEN
    return (request, lookup(lengths, request) + token_index % QLEN)


def key_meta(row_index, layout, permutation, lengths):
    cache_rows, block_size, tok_dev, max_blocks = layout
    rows_dev = cache_rows + tok_dev
    device = row_index // rows_dev
    local_row = row_index % rows_dev
    block_index = (
        device * (cache_rows // block_size) + jnp.minimum(local_row, cache_rows - 1) // block_size
    )
    logical = lookup(permutation, block_index)
    request = logical // max_blocks
    position = logical % max_blocks * block_size + local_row % block_size
    cached_live = position < lookup(lengths, request)
    new_req, new_pos = query_meta(device * tok_dev + local_row - cache_rows, lengths)
    in_cache = local_row < cache_rows
    key_req = jnp.where(in_cache, jnp.where(cached_live, request, -1), new_req)
    return (key_req, jnp.where(in_cache, position, new_pos))


def attend(softmax_state, queries, query_info, key_rows, value_rows, key_info, head_dim):
    query_req, query_pos = query_info
    key_req, key_pos = key_info
    visible = (key_req[None, :] == query_req[:, None]) & (key_pos[None, :] <= query_pos[:, None])
    query_count = queries.shape[0]
    key_count = key_rows.shape[0]
    head_count = queries.shape[1] // head_dim
    summed, largest, weight_sum = softmax_state
    scores = jnp.einsum(
        "qhd,khd->hqk",
        queries.reshape(query_count, head_count, head_dim),
        key_rows.reshape(key_count, head_count, head_dim),
        preferred_element_type=jnp.float32,
    ) * head_dim ** (-0.5)
    scores = jnp.where(visible[None], scores, lowest)
    new_largest = jnp.maximum(largest, jnp.max(scores, axis=-1))
    weights = jnp.where(visible[None], jnp.exp(scores - new_largest[..., None]), 0.0)
    weight_sum = jnp.sum(weights, axis=-1)
    summed = jnp.einsum(
        "hqk,khd->hqd",
        weights.astype(jnp.bfloat16),
        value_rows.reshape(key_count, head_count, head_dim),
        preferred_element_type=jnp.float32,
    )
    return (summed, new_largest, weight_sum)


def per_device(
    inputs,
    norm_gain,
    qkv_weight,
    adapter_down,
    adapter_up,
    out_weight,
    cache_keys,
    cache_values,
    cache_lengths,
    block_perm,
):
    tok_dev = inputs.shape[0]
    widened = inputs.astype(jnp.float32)
    normed = (
        widened * lax.rsqrt(jnp.mean(widened * widened, axis=-1, keepdims=True) + 1e-05) * norm_gain
    ).astype(jnp.bfloat16)
    head_width = qkv_weight.shape[2]
    weight_rows = lax.all_gather(qkv_weight, "seq", axis=0, tiled=True)
    down_rows = lax.all_gather(adapter_down, "seq", axis=0, tiled=True)
    main_part = jnp.einsum("tr,rkc->ktc", normed, weight_rows, preferred_element_type=jnp.float32)
    low_rank = jnp.dot(normed, down_rows, preferred_element_type=jnp.float32)
    main_part, low_rank = (main_part, low_rank)
    low_rank = low_rank.astype(jnp.bfloat16)
    projected = (
        main_part
        + jnp.einsum("tr,krc->ktc", low_rank, adapter_up, preferred_element_type=jnp.float32)
    ).astype(jnp.bfloat16)
    queries = projected[0]
    new_keys = projected[1]
    new_values = projected[2]
    cycle_index = lax.axis_index("seq")
    cache_rows = cache_keys.shape[0] * cache_keys.shape[1]
    layout = (cache_rows, cache_keys.shape[1], tok_dev, block_perm.shape[0] // REQS)
    key_rows = jnp.concatenate([cache_keys.reshape(cache_rows, head_width), new_keys], axis=0)
    value_rows = jnp.concatenate([cache_values.reshape(cache_rows, head_width), new_values], axis=0)
    token_ids = jnp.arange(tok_dev, dtype=jnp.int32)
    own_info = query_meta(cycle_index * tok_dev + token_ids, cache_lengths)
    head_count = head_width // HD
    softmax_state = (
        jnp.zeros((head_count, tok_dev, HD), jnp.float32),
        jnp.full((head_count, tok_dev), lowest, jnp.float32),
        jnp.zeros((head_count, tok_dev), jnp.float32),
    )
    pieces = (
        lax.all_gather(key_rows, "seq", axis=0, tiled=True),
        lax.all_gather(value_rows, "seq", axis=0, tiled=True),
    )
    row_ids = jnp.arange(pieces[0].shape[0], dtype=jnp.int32)
    key_info = key_meta(row_ids, layout, block_perm, cache_lengths)
    softmax_state = attend(softmax_state, queries, own_info, pieces[0], pieces[1], key_info, HD)
    summed, largest, weight_sum = softmax_state
    attended = (
        (summed / weight_sum[..., None])
        .transpose(1, 0, 2)
        .reshape(tok_dev, head_width)
        .astype(jnp.bfloat16)
    )
    partial_value = jnp.dot(
        attended,
        lax.all_gather(out_weight, "seq", axis=1, tiled=True),
        preferred_element_type=jnp.float32,
    )
    return lax.psum_scatter(
        partial_value.astype(jnp.bfloat16), "mp", scatter_dimension=1, tiled=True
    )


CHUNK = 256
GROUP = 128
RANK = 128
LOG2E = 1.4426950408889634


def swap(array, axis, size, bit):
    return lax.ppermute(array, axis, [(i, i ^ bit) for i in range(size)])


def pick(array, index, axis=0):
    return lax.dynamic_index_in_dim(array, index, axis, keepdims=False)


def after(array, *earlier):
    return lax.optimization_barrier((array, *earlier))[0]


def fence(*arrays):
    return lax.optimization_barrier(arrays)


def norm_kernel(first, inputs_ref, gain_ref, out_ref):
    widened = inputs_ref[...].astype(jnp.float32)
    mean = jnp.mean(widened * widened, axis=-1, keepdims=True)
    out_ref[...] = (widened * lax.rsqrt(mean + 1e-05) * gain_ref[...]).astype(jnp.bfloat16)


def normalise(inputs, norm_gain, part, count):
    width = inputs.shape[1]
    rows = 64
    steps = count // rows
    return pl.pallas_call(
        norm_kernel,
        grid_spec=pltpu.PrefetchScalarGridSpec(
            num_scalar_prefetch=1,
            grid=(steps,),
            in_specs=[
                pl.BlockSpec((rows, width), lambda i, first: (first[0] * steps + i, 0)),
                pl.BlockSpec((1, width), lambda i, first: (0, 0)),
            ],
            out_specs=pl.BlockSpec((rows, width), lambda i, first: (i, 0)),
        ),
        out_shape=jax.ShapeDtypeStruct((count, width), jnp.bfloat16),
        compiler_params=pltpu.CompilerParams(vmem_limit_bytes=40 * 2**20),
        cost_estimate=pl.CostEstimate(flops=1, bytes_accessed=1, transcendentals=0),
    )(part.reshape(1), inputs, norm_gain.reshape(1, width))


def project_kernel(sets, order, up_ref, down_ref, *refs):
    token_refs, weight_refs = refs[: len(sets)], refs[len(sets) : -3]
    turned_ref, keys_ref, held_ref = refs[-3:]
    rows = weight_refs[0].shape[1]
    main = 3 * HD
    step = pl.program_id(0)

    @pl.when(step == 0)
    def fill():
        for number, weight_ref in enumerate(weight_refs):
            columns = pl.ds(pl.multiple_of(order[number] * rows, 128), rows)
            held_ref[pl.ds(0, main), columns] = weight_ref[...]
        held_ref[pl.ds(main, RANK), :] = down_ref[...]

    def run(tokens_ref):
        total = lax.dot_general(
            held_ref[...],
            tokens_ref[...],
            (((1,), (1,)), ((), ())),
            preferred_element_type=jnp.float32,
        )
        low_rank = total[main:].astype(jnp.bfloat16)
        total = total[:main] + jnp.dot(up_ref[...], low_rank, preferred_element_type=jnp.float32)
        for number in range(turned_ref.shape[0]):
            columns = slice(number * CHUNK, (number + 1) * CHUNK)
            turned_ref[number, pl.ds(0, HD), :] = total[:HD, columns].astype(jnp.bfloat16)
            turned_ref[number, pl.ds(HD, HD), :] = total[2 * HD :, columns].astype(jnp.bfloat16)
            keys_ref[number] = total[HD : 2 * HD, columns].T.astype(jnp.bfloat16)

    for (first, count), tokens_ref in zip(sets, token_refs):
        pl.when((step >= first) & (step < first + count))(functools.partial(run, tokens_ref))


def project(token_sets, up, down, weight_blocks, order):
    width = token_sets[0].shape[1]
    per_step = 1 if len(token_sets) > 1 else 2
    main = 3 * HD
    sets, steps = [], 0
    for tokens in token_sets:
        sets.append((steps, tokens.shape[0] // (per_step * CHUNK)))
        steps += sets[-1][1]
    chunks = steps * per_step
    whole = lambda array: pl.BlockSpec(array.shape, lambda i, *_: (0,) * array.ndim)

    def token_spec(first, count):
        return pl.BlockSpec(
            (per_step * CHUNK, width), lambda i, *_: (jnp.clip(i - first, 0, count - 1), 0)
        )

    return pl.pallas_call(
        functools.partial(project_kernel, tuple(sets)),
        grid_spec=pltpu.PrefetchScalarGridSpec(
            num_scalar_prefetch=1,
            grid=(steps,),
            in_specs=[whole(array) for array in (up, down)]
            + [token_spec(*one) for one in sets]
            + [
                pl.BlockSpec(
                    (main, array.shape[1]), lambda i, *_: (0, 0), pipeline_mode=pl.Buffered(1)
                )
                for array in weight_blocks
            ],
            out_specs=[
                pl.BlockSpec((per_step, 2 * HD, CHUNK), lambda i, *_: (i, 0, 0)),
                pl.BlockSpec((per_step, CHUNK, HD), lambda i, *_: (i, 0, 0)),
            ],
            scratch_shapes=[pltpu.VMEM((main + RANK, width), jnp.bfloat16)],
        ),
        out_shape=[
            jax.ShapeDtypeStruct((chunks, 2 * HD, CHUNK), jnp.bfloat16),
            jax.ShapeDtypeStruct((chunks, CHUNK, HD), jnp.bfloat16),
        ],
        compiler_params=pltpu.CompilerParams(vmem_limit_bytes=58 * 2**20),
        cost_estimate=pl.CostEstimate(flops=1, bytes_accessed=1, transcendentals=0),
    )(order, up, down, *token_sets, *weight_blocks)


def attention_kernel(
    half,
    chunk_table,
    cache_table,
    length_ref,
    turned_ref,
    keys_ref,
    *refs,
):
    block_refs, (out_ref, total_ref, cached_keys, cached_values) = refs[:-4], refs[-4:]
    tile = 2 * pl.program_id(0) + half
    factor = HD ** (-0.5) * LOG2E
    width = 2 * CHUNK
    length = length_ref[0]

    @pl.when(pl.program_id(0) == 0)
    def gather_cache():
        for number in range(cache_table.shape[0]):
            entry = cache_table[number]

            @pl.when(number * CHUNK >= length)
            def clear(number=number):
                place = pl.ds(number * CHUNK, CHUNK)
                cached_values[:, place] = jnp.zeros((HD, CHUNK), jnp.bfloat16)

            for bit, block_ref in enumerate(block_refs):

                @pl.when((number * CHUNK < length) & (entry // 4 == bit))
                def take(number=number, entry=entry, block_ref=block_ref):
                    other = (entry // 2) % 2
                    columns = pl.ds(pl.multiple_of((entry % 2) * CHUNK, CHUNK), CHUNK)
                    place = pl.ds(number * CHUNK, CHUNK)
                    keys = block_ref[other, pl.ds(0, HD), columns].astype(jnp.float32)
                    cached_keys[place, :] = keys.T.astype(jnp.bfloat16)
                    cached_values[:, place] = block_ref[other, pl.ds(HD, HD), columns]

    def joined(ref, first, rows):
        pieces = [ref[chunk_table[first + place], rows, :] for place in range(2)]
        return jnp.concatenate(pieces, axis=1)

    query_rows, value_rows = pl.ds(0, HD), pl.ds(HD, HD)
    queries = joined(turned_ref, 2 * tile, query_rows)

    def step(state, keys, values, visible):
        largest, weight_sum = state
        scores = jnp.dot(keys, queries, preferred_element_type=jnp.float32)
        if visible is not None:
            scores = jnp.where(visible, scores, lowest)
        new_largest = jnp.maximum(largest, jnp.max(scores, axis=0, keepdims=True))
        weights = jnp.exp2((scores - new_largest) * factor)
        fade = jnp.exp2((largest - new_largest) * factor)
        weight_sum = weight_sum * fade + jnp.sum(weights, axis=0, keepdims=True)
        total_ref[...] = total_ref[...] * fade + jnp.dot(
            values, weights.astype(jnp.bfloat16), preferred_element_type=jnp.float32
        )
        return (new_largest, weight_sum)

    def new_step(number, state, visible=None):
        first = 2 * number
        pieces = [keys_ref[chunk_table[first + place]] for place in range(2)]
        keys = jnp.concatenate(pieces, axis=0)
        return step(state, keys, joined(turned_ref, first, value_rows), visible)

    def cache_step(number, state):
        place = pl.ds(pl.multiple_of(number * width, width), width)
        visible = key_row + number * width < length
        return step(state, cached_keys[place, :], cached_values[:, place], visible)

    total_ref[...] = jnp.zeros_like(total_ref)
    state = (jnp.full((1, width), lowest, jnp.float32), jnp.zeros((1, width), jnp.float32))
    key_row = lax.broadcasted_iota(jnp.int32, (width, width), 0)
    query_column = lax.broadcasted_iota(jnp.int32, (width, width), 1)
    state = new_step(tile, state, key_row <= query_column)
    state = lax.fori_loop(0, tile, new_step, state)
    state = lax.fori_loop(0, pl.cdiv(length, width), cache_step, state)
    out_ref[...] = (total_ref[...] / state[1]).astype(jnp.bfloat16)


def attention(half, turned, keys, cache_blocks, chunk_table, cache_table, length):
    whole = lambda array: pl.BlockSpec(array.shape, lambda i, *_: (0, 0, 0))
    cache_span = cache_table.shape[0] * CHUNK
    return pl.pallas_call(
        functools.partial(attention_kernel, half),
        grid_spec=pltpu.PrefetchScalarGridSpec(
            num_scalar_prefetch=3,
            grid=(QLEN // (4 * CHUNK),),
            in_specs=[whole(array) for array in (turned, keys, *cache_blocks)],
            out_specs=pl.BlockSpec((HD, 2 * CHUNK), lambda i, *_: (0, i)),
            scratch_shapes=[
                pltpu.VMEM((HD, 2 * CHUNK), jnp.float32),
                pltpu.VMEM((cache_span, HD), jnp.bfloat16),
                pltpu.VMEM((HD, cache_span), jnp.bfloat16),
            ],
        ),
        out_shape=jax.ShapeDtypeStruct((HD, QLEN // 2), jnp.bfloat16),
        compiler_params=pltpu.CompilerParams(vmem_limit_bytes=48 * 2**20),
        cost_estimate=pl.CostEstimate(flops=1, bytes_accessed=1, transcendentals=0),
    )(chunk_table, cache_table, length, turned, keys, *cache_blocks)


def per_device_paired(
    inputs,
    norm_gain,
    qkv_weight,
    adapter_down,
    adapter_up,
    out_weight,
    cache_keys,
    cache_values,
    cache_lengths,
    block_perm,
):
    tok_dev, width = inputs.shape
    rows = qkv_weight.shape[0]
    plane, side = lax.axis_index("z"), lax.axis_index("x")
    row, core = lax.axis_index("y"), lax.axis_index("core")
    seq, mp = 2 * plane + side, 2 * row + core
    role = plane % 2

    def over_z(array, bit):
        return swap(array, "z", 4, bit)

    def over_x(array):
        return swap(array, "x", 2, 1)

    def over_y(array):
        return swap(array, "y", 2, 1)

    def over_core(array):
        return swap(array, "core", 2, 1)

    part = normalise(inputs, norm_gain, mp, CHUNK)
    plane_axes = ("x", "y", "core")
    plane_axes = ("x", "y", "core")
    part_z = over_z(part, 1)
    part_x = over_x(part)

    turned = qkv_weight.reshape(rows, 3, 4, HD).transpose(2, 1, 3, 0).reshape(2, 2, 3 * HD, rows)
    kept = pick(turned, side, 1)
    given = pick(turned, 1 - side, 1)
    from_x = over_x(jnp.stack([pick(given, role), pick(given, 1 - role)]))
    kept_near = pick(kept, 1 - role)
    far = {bit: [over_z(pick(kept, role ^ (bit & 1)), bit)] for bit in (2, 3)}
    share = lax.dynamic_slice_in_dim(adapter_down, mp * (rows // 4), rows // 4, 0)
    down = lax.all_gather(share, ("z", "x", "y", "core"), axis=0, tiled=True)

    def turned_cache(cache):
        blocks, size, _ = cache.shape
        return cache.reshape(blocks * size, 4, HD).transpose(1, 2, 0)

    cached = jnp.concatenate([turned_cache(cache_keys), turned_cache(cache_values)], axis=1)
    cached = cached.reshape(2, 2, 2 * HD, cached.shape[2])

    near_rows = jnp.stack([kept_near, from_x[1]])
    same_rows, other_rows = from_x[0], from_x[1]
    cache_own, cache_given = pick(cached, side, 1), pick(cached, 1 - side, 1)
    (
        part_z,
        part_x,
        near_rows,
        same_rows,
        other_rows,
        far[2][0],
        far[3][0],
        cache_own,
        cache_given,
        down,
        inputs,
    ) = fence(
        part_z,
        part_x,
        near_rows,
        same_rows,
        other_rows,
        far[2][0],
        far[3][0],
        cache_own,
        cache_given,
        down,
        inputs,
    )
    pair_tokens = lax.all_gather(part_z, plane_axes, axis=0, tiled=True)
    near = over_z(near_rows, 1)
    far[2].append(over_z(same_rows, 2))
    far[3].append(over_z(other_rows, 3))
    cache_from_x = over_x(cache_given)
    core_x = over_core(part_x)
    normed = normalise(inputs, norm_gain, jnp.int32(0), tok_dev)
    down = down.T

    start = (mp ^ 2) * CHUNK + GROUP
    given_x = lax.dynamic_slice_in_dim(normed, start, GROUP, 0)
    given_y = part_x[:GROUP]
    cache_both = jnp.stack([cache_own, cache_from_x], axis=1)
    cache_same, cache_other = pick(cache_both, role), pick(cache_both, 1 - role)
    near, far[2][1], far[3][1], cache_same, cache_other, core_x, normed, part_x = fence(
        near, far[2][1], far[3][1], cache_same, cache_other, core_x, normed, part_x
    )
    given_x, given_y, down, part_x = fence(given_x, given_y, down, part_x)
    cache_blocks = [
        cache_same,
        over_z(cache_other, 1),
        over_z(cache_same, 2),
        over_z(cache_other, 3),
    ]
    part_y = over_y(given_y)
    part_yx = over_x(given_x)
    weight_blocks = [pick(kept, role), same_rows, near[0], near[1], *far[2], *far[3]]
    order = jnp.arange(8, dtype=jnp.int32) ^ seq
    up = adapter_up.reshape(3, RANK, 4, HD).transpose(2, 0, 3, 1).reshape(4, 3 * HD, RANK)
    up = pick(up, 2 * role + side)

    requests = jnp.stack([plane, plane ^ 1])
    lengths = lookup(cache_lengths, requests)
    logical = requests[:, None] * 4 + jnp.arange(4, dtype=jnp.int32)[None, :]
    hits = logical[..., None] == block_perm
    physical = jnp.sum(
        jnp.where(hits, jnp.arange(block_perm.shape[0], dtype=jnp.int32), 0), axis=-1
    )
    cache_table = (((physical // 2) ^ seq) * 2 + physical % 2).astype(jnp.int32)

    def attend(number, half, projected):
        turned_rows, key_rows = projected
        return attention(
            half,
            turned_rows,
            key_rows,
            cache_blocks,
            chunk_tables[number],
            cache_table[number],
            lengths[number : number + 1],
        )

    half_dev = tok_dev // 2

    place = jnp.arange(8, dtype=jnp.int32)
    moved = (place % 4) ^ mp
    chunk_tables = (
        jnp.where(place // 4 == side, place % 4, 4 + moved),
        place,
    )
    local_projected = project((normed, part_x, core_x), up, down, weight_blocks, order)

    *cache_blocks, up, local_turned, local_keys, out_weight, part_y, part_yx = fence(
        *cache_blocks, up, *local_projected, out_weight, part_y, part_yx
    )
    part_y = jnp.concatenate([part_y, part_yx])
    core_y = over_core(part_y)
    pair_projected = project((pair_tokens,), up, down, weight_blocks, order)
    pair_first = attend(1, 0, pair_projected)
    pair_first, pair_turned, core_y, up = fence(pair_first, pair_projected[0], core_y, up)

    out_rows = lax.all_gather(out_weight, ("z", "x"), axis=1, tiled=True)
    out_cols = out_rows.shape[1] // 4

    def out_columns(to_row, to_core):
        return lax.dynamic_slice_in_dim(out_rows, (2 * to_row + to_core) * out_cols, out_cols, 1)

    columns = {
        "away_core": out_columns(1 - row, 1 - core),
        "away": out_columns(1 - row, core),
        "here_core": out_columns(row, 1 - core),
        "here": out_columns(row, core),
    }

    def rounded(array):
        return array.astype(jnp.bfloat16)

    def out_part(heads, name):
        return lax.dot_general(
            heads, columns[name], (((0,), (0,)), ((), ())), preferred_element_type=jnp.float32
        )

    def summed(heads):
        away = over_core(rounded(out_part(heads, "away_core")))
        here = over_core(rounded(out_part(heads, "here_core")))
        away = rounded(out_part(heads, "away") + away.astype(jnp.float32))
        return away, out_part(heads, "here") + here.astype(jnp.float32)

    def crossing(attended):
        return lax.dynamic_slice_in_dim(attended, (1 - side) * half_dev, half_dev, 1)

    def both_sides(attended, theirs):
        mine = lax.dynamic_slice_in_dim(attended, side * half_dev, half_dev, 1)
        return jnp.where(side == 0, jnp.stack([mine, theirs]), jnp.stack([theirs, mine]))

    def all_heads(own, own_theirs, pair, pair_theirs):
        own_heads, pair_heads = both_sides(own, own_theirs), both_sides(pair, pair_theirs)
        return jnp.where(
            role == 0,
            jnp.concatenate([own_heads, pair_heads]),
            jnp.concatenate([pair_heads, own_heads]),
        ).reshape(4 * HD, half_dev)

    pair_first = over_z(pair_first, 1)
    parts_turned, parts_keys = project((part_y, core_y), up, down, weight_blocks, order)
    own_keys = jnp.concatenate([local_keys, parts_keys])
    own_turned = jnp.concatenate([local_turned, parts_turned])
    pair_second = attend(1, 1, (pair_turned, pair_projected[1]))
    pair_first, pair_second, own_turned, own_keys = fence(
        pair_first, pair_second, own_turned, own_keys
    )
    pair_first_crossed = over_x(crossing(pair_first))
    pair_second = over_z(pair_second, 1)
    own_first = attend(0, 0, (own_turned, own_keys))
    pair_first_crossed, own_first, own_turned = fence(pair_first_crossed, own_first, own_turned)
    own_first_crossed = over_x(crossing(own_first))
    first_sent, first_here = summed(
        all_heads(own_first, own_first_crossed, pair_first, pair_first_crossed)
    )
    pair_second, first_sent, first_here, own_turned = fence(
        pair_second, first_sent, first_here, own_turned
    )
    first_received = over_y(first_sent)
    pair_second_crossed = over_x(crossing(pair_second))
    own_second = attend(0, 1, (own_turned, own_keys))
    pair_second_crossed, own_second = fence(pair_second_crossed, own_second)
    own_second_crossed = over_x(crossing(own_second))
    own_second_crossed, first_received = fence(own_second_crossed, first_received)
    second_sent, second_here = summed(
        all_heads(own_second, own_second_crossed, pair_second, pair_second_crossed)
    )
    second_received = over_y(second_sent)
    return jnp.concatenate(
        [
            rounded(first_here + first_received.astype(jnp.float32)),
            rounded(second_here + second_received.astype(jnp.float32)),
        ]
    )


def solution(mesh):
    paired = mesh.shape["seq"] == 8 and mesh.shape["mp"] == 4
    if paired:
        seq, mp = ("z", "x"), ("y", "core")
        mesh = jax.sharding.Mesh(mesh.devices.reshape(4, 2, 2, 2), seq + mp)
    else:
        seq, mp = "seq", "mp"
    in_specs = (
        P(seq, None),
        P(),
        P(seq, None, mp),
        P(seq, None),
        P(None, None, mp),
        P(mp, seq),
        P(seq, None, mp),
        P(seq, None, mp),
        P(),
        P(),
    )
    return jax.shard_map(
        per_device_paired if paired else per_device,
        mesh=mesh,
        in_specs=in_specs,
        out_specs=P(seq, mp),
        check_vma=False,
    )
```
